256 devices in a mesh: tile: 4 (over z_hi, core), epoch: 64 (over x, z_lo, y).
Axes of the slice: x: 4, y: 4, z: 8 (z_hi: 2, z_lo: 4; z = z_hi * 4 + z_lo), core: 2. Of those that a mesh axis runs over, the one named last changes fastest.
Arguments:
- coadd_image: float32 [4, 512, 1024], P('tile', 'epoch'), may hold values from -6 to 6
- science: float32 [4, 64, 256, 256], P('tile', 'epoch'), may hold values from -6 to 14
- row_offset: int32 [4, 64], P('tile', 'epoch'), may hold values from 15 to 241
- col_offset: int32 [4, 64], P('tile', 'epoch'), may hold values from 15 to 753
- intersections: int32 [4, 64], P('tile', 'epoch'), may hold values 0 or 1
- visit_weight: float32 [4, 64], P('tile', 'epoch'), may hold values from 0.25 to 4
- basis_index: int32 [4, 64, 2, 3, 2], P('tile', 'epoch'), may hold values from 0 to 15
- weights: float32 [4, 64, 2, 2, 3], P('tile', 'epoch'), may hold values from 0.3 to 1.5
- profiles: float32 [16, 31], replicated, may hold values from -1 to 1
Outputs:
- mean_difference: float32 [4, 512, 1024], P('tile', 'epoch')
The draws below stay inside these ranges and needn't reach their ends.
All inputs are finite; a program needn't handle non-finite values. No bound on the sum of `intersections` on one device may be relied on, other than what follows from the above.
Results may differ from the reference program's by a relative error of at most 0.0003.
Values sent between devices are 32-bit elements; how exact they have to be, the bound alone decides.
A program may use at most 64 MiB of HBM per device.

```python
import math
import jax
import jax.numpy as jnp
from jax import lax

TH = 512
TW = 1024
WH = 256
WW = 256
KW = 31
RW = 128
B = 3
NPROF = 16
NT = 4
EPOCHS = 64
NRX = 2
NRY = 2


def draw_science(key, part):
    noise_key = jax.random.fold_in(key, 11)
    level_key = jax.random.fold_in(key, 12)
    noise = jnp.clip(jax.random.normal(noise_key, (NT, EPOCHS, WH, WW), jnp.float32), -6.0, 6.0)
    factor = jax.random.uniform(level_key, (1, EPOCHS, 1, 1), jnp.float32, 0.5, 1.5)
    ladder = (1.0 + jnp.arange(NT, dtype=jnp.float32)).reshape(NT, 1, 1, 1)
    return noise + ladder * factor


def set_ends(values, rng, least, high):
    longest = values.shape.index(max(values.shape))
    spots = []
    for shift in (0, 1):
        where = [jax.random.randint(jax.random.fold_in(rng, axis), (), 0, length) for axis, length in enumerate(values.shape)]
        where[longest] = (where[longest] + shift) % values.shape[longest]
        spots.append(tuple(where))
    return values.at[spots[0]].set(least).at[spots[1]].set(high)


def steps_of(own_key, extent, shards, smallest, high):
    def one(position, blocks):
        draws = jax.random.uniform(jax.random.fold_in(jax.random.fold_in(own_key, 6), position), (blocks,), jnp.float32, smallest / len(shards), high / len(shards))
        return jnp.repeat(jnp.exp(draws), extent[position] // blocks).reshape((-1,) + (1,) * (len(extent) - position - 1))

    level = one(*shards[0])
    for cut in shards[1:]:
        level = level * one(*cut)
    return level


def gaussian(rng, extent, scale, reach, split=(), kind=jnp.bfloat16):
    values = scale * jax.random.normal(rng, extent, jnp.float32)
    if split:
        values = values * steps_of(rng, extent, split, -0.22, 0.18)
    return jnp.clip(values, -reach, reach).astype(kind)


def setup_inputs(seed: int = 0) -> dict:
    keys = jax.random.split(jax.random.key(seed), 10)
    return {
        "coadd_image": gaussian(keys[0], (NT, TH, TW), 1.0, 6.0, ((0, 4), (1, 64)), jnp.float32),
        "science": draw_science(jax.random.fold_in(keys[9], 71), 0),
        "row_offset": set_ends(jax.random.randint(keys[2], (NT, EPOCHS), (KW - 1) // 2, TH - WH - (KW - 1) // 2 + 1), jax.random.fold_in(keys[2], 1), (KW - 1) // 2, (TH - WH - (KW - 1) // 2 + 1) - 1).astype(jnp.int32),
        "col_offset": set_ends(jax.random.randint(keys[3], (NT, EPOCHS), (KW - 1) // 2, TW - WW - (KW - 1) // 2 + 1), jax.random.fold_in(keys[3], 1), (KW - 1) // 2, (TW - WW - (KW - 1) // 2 + 1) - 1).astype(jnp.int32),
        "intersections": set_ends((jax.random.randint(keys[4], (NT, EPOCHS), 0, 2) < 1).astype(jnp.int32), jax.random.fold_in(keys[4], 1), 0, 1),
        "visit_weight": jnp.clip(jnp.exp(math.log(4.0) - 2.7725887 * jax.random.uniform(keys[5], (NT, EPOCHS), jnp.float32) ** steps_of(keys[5], (NT, EPOCHS), ((0, 4), (1, 64)), -0.2, 0.2)), 0.25, 4.0),
        "basis_index": set_ends(jax.random.randint(keys[6], (NT, EPOCHS, NRX, B, 2), 0, NPROF), jax.random.fold_in(keys[6], 1), 0, NPROF - 1).astype(jnp.int32),
        "weights": jnp.clip(0.3 + 1.2 * jax.random.uniform(keys[7], (NT, EPOCHS, NRY, NRX, B), jnp.float32) ** steps_of(keys[7], (NT, EPOCHS, NRY, NRX, B), ((0, 4), (1, 64)), -0.2, 0.2), 0.3, 1.5),
        "profiles": gaussian(keys[8], (NPROF, KW), KW ** -0.5, 1.0, (), jnp.float32),
    }


def expand_taps(index, profiles):
    chosen = profiles[index]
    return jnp.repeat(chosen, RW, axis=0)


def convolve(window_in, index_pair, weight_map, profiles):
    horizontal = expand_taps(index_pair[:, :, 0], profiles)
    vertical = expand_taps(index_pair[:, :, 1], profiles)
    result = jnp.zeros((WH, WW), jnp.float32)
    for basis_id in range(B):
        across = jnp.zeros((WH + KW - 1, WW), jnp.float32)
        for offset in range(KW):
            across = across + horizontal[:, basis_id, offset][None, :] * window_in[:, offset:offset + WW]
        downward = jnp.zeros((WH, WW), jnp.float32)
        for offset in range(KW):
            downward = downward + vertical[:, basis_id, offset][None, :] * across[offset:offset + WH, :]
        scale_map = jnp.repeat(jnp.repeat(weight_map[:, :, basis_id], RW, axis=0), RW, axis=1)
        result = result + scale_map * downward
    return result


def reference(coadd_image, science, row_offset, col_offset, intersections, visit_weight, basis_index, weights, profiles):
    half_width = (KW - 1) // 2

    def residual_of(flat_index):
        tile_id = (flat_index // EPOCHS).astype(jnp.int32)
        epoch_id = (flat_index % EPOCHS).astype(jnp.int32)
        row_start = (row_offset[tile_id, epoch_id] - half_width).astype(jnp.int32)
        col_start = (col_offset[tile_id, epoch_id] - half_width).astype(jnp.int32)
        window_in = lax.dynamic_slice(coadd_image, (tile_id, row_start, col_start), (1, WH + KW - 1, WW + KW - 1))[0]
        model = convolve(window_in, basis_index[tile_id, epoch_id], weights[tile_id, epoch_id], profiles)
        return science[tile_id, epoch_id] - model

    residual = lax.map(residual_of, jnp.arange(NT * EPOCHS, dtype=jnp.int32)).reshape(NT, EPOCHS, WH, WW)
    flags = intersections.astype(jnp.float32)
    visit_sums = jnp.sum(residual, axis=(2, 3)) * flags
    visit_count = flags * float(WH * WW)
    level = jnp.sum(visit_sums, axis=0) / jnp.maximum(jnp.sum(visit_count, axis=0), 1.0)

    def place(carry, flat_index):
        total_sum, coverage = carry
        tile_id = (flat_index // EPOCHS).astype(jnp.int32)
        epoch_id = (flat_index % EPOCHS).astype(jnp.int32)
        row_start = row_offset[tile_id, epoch_id].astype(jnp.int32)
        col_start = col_offset[tile_id, epoch_id].astype(jnp.int32)
        gain = flags[tile_id, epoch_id] * visit_weight[tile_id, epoch_id]
        difference = (residual[tile_id, epoch_id] - level[epoch_id]) * gain
        corner = (tile_id, row_start, col_start)
        region = lax.dynamic_slice(total_sum, corner, (1, WH, WW))
        total_sum = lax.dynamic_update_slice(total_sum, region + difference[None], corner)
        region = lax.dynamic_slice(coverage, corner, (1, WH, WW))
        coverage = lax.dynamic_update_slice(coverage, region + gain * jnp.ones((1, WH, WW), jnp.float32), corner)
        return (total_sum, coverage), None

    start = (jnp.zeros((NT, TH, TW), jnp.float32), jnp.zeros((NT, TH, TW), jnp.float32))
    (total_sum, coverage), unused = lax.scan(place, start, jnp.arange(NT * EPOCHS, dtype=jnp.int32))
    return total_sum / jnp.maximum(coverage, 1.0)
```

```python
import jax
import jax.numpy as jnp
from jax import lax
from jax.experimental import pallas as pl
from jax.experimental.pallas import tpu as pltpu
from jax.sharding import PartitionSpec as P

KW = 31
HALF = 15
RW = 128
B = 3
F32 = jnp.float32
BF16 = jnp.bfloat16
MESH = pl.DeviceIdType.MESH

STRIDES = (16, 4, 1)
PARTS = (
    (0, 384, (1, 2, 0)),
    (384, 384, (1, 0, 2)),
    (768, 256, (2, 0, 1)),
)
NPART = len(PARTS)
ROWS = 512
COLS = 512


def split(value):
    high = value.astype(BF16)
    return high, (value - high.astype(F32)).astype(BF16)


def dot3(a_high, a_low, b_high, b_low):
    def dot(a, b):
        return jnp.dot(a, b, preferred_element_type=F32)

    return dot(a_high, b_high) + (dot(a_high, b_low) + dot(a_low, b_high))


def roll_by(value, amount, axis):
    chosen = jnp.broadcast_to(amount, value.shape)
    step = 1
    while step < value.shape[axis]:
        value = jnp.where((chosen & step) != 0, pltpu.roll(value, step, axis), value)
        step *= 2
    return value


def toeplitz(taps, shift, rows):
    width = taps.shape[1]
    base = roll_by(jnp.broadcast_to(taps, (8, width)), shift, 1)
    return pltpu.roll(jnp.broadcast_to(base[0:1, :], (rows, width)), 0, 1, stride=1, stride_axis=0)


def kernel(
    coadd, science, row_offset, col_offset, intersections, visit_weight, basis_index, weights, profiles,
    out,
    tile, sci, table, hor_hi, hor_lo, ver_hi, ver_lo, slots, recv, info, infos, cover, offs, levels, sums,
    local_sem, send_sem, recv_sem, info_send, info_recv, sum_send, sum_recv, a2a_sem, lev_sem,
):
    me_t = lax.axis_index("tile")
    me = lax.axis_index("epoch")
    coord = (me // 16, (me // 4) % 4, me % 4)

    own_copy = pltpu.make_async_copy(coadd.at[0], tile.at[coord[0], coord[1], coord[2]], local_sem.at[0])
    own_copy.start()
    sci_copy = pltpu.make_async_copy(science.at[0, 0], sci, local_sem.at[1])
    sci_copy.start()

    def peer(axis, k):
        here = coord[axis]
        return me + (lax.rem(here + k, 4) - here) * STRIDES[axis]

    barrier = pltpu.get_barrier_semaphore()
    for axis in range(3):
        for k in (1, 2, 3):
            pl.semaphore_signal(barrier, inc=1, device_id={"epoch": peer(axis, k)}, device_id_type=MESH)
    for k in (1, 2, 3):
        pl.semaphore_signal(barrier, inc=1, device_id={"tile": lax.rem(me_t + k, 4)}, device_id_type=MESH)

    oy = row_offset[0, 0]
    ox = col_offset[0, 0]
    flag = intersections[0, 0].astype(F32)
    gain = flag * visit_weight[0, 0]
    lane = lax.broadcasted_iota(jnp.int32, (1, 128), 1)
    info[coord[0], coord[1], coord[2]] = jnp.where(
        lane == 0, oy.astype(F32), jnp.where(lane == 1, ox.astype(F32), gain)
    )
    own_copy.wait()
    pl.semaphore_wait(barrier, 12)

    def stage_copies(buffer, cols, order, stage, sends, recvs):
        axis = order[stage]
        where = tuple(slice(None) if a in order[:stage] else coord[a] for a in range(3))
        block = buffer.at[where + ((slice(None),) if cols is None else (slice(None), pl.ds(*cols)))]
        return [
            pltpu.make_async_remote_copy(
                src_ref=block,
                dst_ref=block,
                send_sem=sends.at[k - 1],
                recv_sem=recvs.at[k - 1],
                device_id={"epoch": peer(axis, k)},
                device_id_type=MESH,
            )
            for k in (1, 2, 3)
        ]

    def part_copies(part, stage):
        lo, width, order = PARTS[part]
        return stage_copies(tile, (lo, width), order, stage, send_sem.at[part, stage], recv_sem.at[part, stage])

    def info_copies(stage):
        return stage_copies(info, None, (1, 2, 0), stage, info_send.at[stage], info_recv.at[stage])

    started = []

    def start_stage(stage):
        for part in range(NPART):
            if stage:
                for copy in part_copies(part, stage - 1):
                    copy.wait_recv()
            for copy in part_copies(part, stage):
                copy.start()
                started.append(copy)
        if stage:
            for copy in info_copies(stage - 1):
                copy.wait_recv()
        for copy in info_copies(stage):
            copy.start()
            started.append(copy)

    start_stage(0)

    row_start = oy - HALF
    col_start = ox - HALF
    col_block = jnp.minimum(col_start >> 7, (1024 - COLS) // 128)
    row_shift = row_start
    col_shift = col_start - 128 * col_block

    table[...] = jnp.zeros_like(table)
    table[:, 0:KW] = profiles[...]

    profile = lax.broadcasted_iota(jnp.int32, (16, COLS), 0)

    def taps_of(index):
        return jnp.sum(jnp.where(profile == index, table[...], 0.0), axis=0, keepdims=True)

    def make_horizontal(s):
        for b in range(B):
            taps = taps_of(basis_index[0, 0, s, b, 0])
            band = toeplitz(taps, col_shift + s * RW, RW).T
            at = (s * B + b) * RW
            hor_hi[:, at : at + RW], hor_lo[:, at : at + RW] = split(band)

    def make_vertical(s):
        for b in range(B):
            taps = taps_of(basis_index[0, 0, s, b, 1])
            band = toeplitz(taps, row_shift, 2 * RW)
            row = lax.broadcasted_iota(jnp.int32, (2 * RW, 1), 0)
            band = band * jnp.where(row < RW, weights[0, 0, 0, s, b], weights[0, 0, 1, s, b])
            ver_hi[s * B + b], ver_lo[s * B + b] = split(band)

    make_horizontal(0)
    start_stage(1)
    make_horizontal(1)
    start_stage(2)
    make_vertical(0)
    make_vertical(1)

    for copy in info_copies(2):
        copy.wait_recv()
    for e in range(64):
        infos[e : e + 1, :] = info[e // 16, (e // 4) % 4, e % 4]
    every = infos[...]
    offs[...] = jnp.broadcast_to(every[:, 0:1], (64, 128))
    column = lax.broadcasted_iota(jnp.int32, (64, 1024), 1).astype(F32)
    first = every[:, 1:2]
    cover[...] = jnp.where((column >= first) & (column < first + 256.0), 1.0, 0.0)

    sci_copy.wait()
    for part in range(NPART):
        for copy in part_copies(part, 2):
            copy.wait_recv()

    window = [tile[:, :, :, :, j * 128 : (j + 1) * 128].reshape(ROWS, 128) for j in range(8)]
    chosen = jnp.broadcast_to(col_block, (ROWS, 128))
    for step in (4, 2, 1):
        keep = COLS // 128 + step - 1
        moved = (chosen & step) != 0
        window = [
            jnp.where(moved, window[j + step], window[j]) if j + step < len(window) else window[j]
            for j in range(min(keep, len(window)))
        ]
    window = jnp.concatenate(window, axis=1)
    win_hi, win_lo = split(window)
    total = jnp.zeros((1, RW), F32)
    for s in range(2):
        across = dot3(
            win_hi, win_lo, hor_hi[:, s * B * RW : (s + 1) * B * RW], hor_lo[:, s * B * RW : (s + 1) * B * RW]
        )
        model = None
        for b in range(B):
            x_hi, x_lo = split(across[:, b * RW : (b + 1) * RW])
            term = dot3(ver_hi[s * B + b], ver_lo[s * B + b], x_hi, x_lo)
            model = term if model is None else model + term
        residual = sci[:, s * RW : (s + 1) * RW] - model
        total = total + jnp.sum(residual, axis=0, keepdims=True)
        sci[:, s * RW : (s + 1) * RW] = residual * gain
    sums[me_t] = jnp.where(
        lax.broadcasted_iota(jnp.int32, (2, RW), 0) == 0, jnp.sum(total) * flag, flag
    )

    sum_copies = [
        pltpu.make_async_remote_copy(
            src_ref=sums.at[me_t],
            dst_ref=sums.at[me_t],
            send_sem=sum_send.at[k - 1],
            recv_sem=sum_recv.at[k - 1],
            device_id={"tile": lax.rem(me_t + k, 4)},
            device_id_type=MESH,
        )
        for k in (1, 2, 3)
    ]
    for copy in sum_copies:
        copy.start()

    folded = roll_by(roll_by(sci[...], ox & 255, 1), oy & 255, 0)
    slots[...] = folded.reshape(32, 8, 256)

    def send_block(k, carry):
        target = lax.rem(me + k, 64)
        pltpu.make_async_remote_copy(
            src_ref=slots.at[lax.rem(target, 32)],
            dst_ref=recv.at[me],
            send_sem=a2a_sem.at[0],
            recv_sem=a2a_sem.at[1],
            device_id={"epoch": target},
            device_id_type=MESH,
        ).start()
        return carry

    lax.fori_loop(1, 64, send_block, 0)
    recv[me] = slots[lax.rem(me, 32)]

    for copy in sum_copies:
        copy.wait_recv()
    residual_sum = sums[0, 0:1, :] + sums[1, 0:1, :] + sums[2, 0:1, :] + sums[3, 0:1, :]
    flags = sums[0, 1:2, :] + sums[1, 1:2, :] + sums[2, 1:2, :] + sums[3, 1:2, :]
    levels[me] = gain * (residual_sum / jnp.maximum(flags * 65536.0, 1.0))

    def send_level(k, carry):
        target = lax.rem(me + k, 64)
        pltpu.make_async_remote_copy(
            src_ref=levels.at[me],
            dst_ref=levels.at[me],
            send_sem=lev_sem.at[0],
            recv_sem=lev_sem.at[1],
            device_id={"epoch": target},
            device_id_type=MESH,
        ).start()
        return carry

    lax.fori_loop(1, 64, send_level, 0)

    for copy in started:
        copy.wait_send()
    for copy in sum_copies:
        copy.wait_send()

    def wait_for(ref, sem):
        pltpu.make_async_copy(ref, ref, sem).wait()

    most = pl.ds(0, 63)
    wait_for(recv.at[most], a2a_sem.at[0])
    wait_for(levels.at[most], lev_sem.at[0])
    wait_for(recv.at[most], a2a_sem.at[1])
    wait_for(levels.at[most], lev_sem.at[1])

    my_row = (me * 8 + lax.broadcasted_iota(jnp.int32, (8, RW), 0)).astype(F32)
    out_blocks = 8

    def add_block(e, carry):
        acc, cnt = carry
        first_row = jnp.broadcast_to(offs[pl.ds(e, 1), :], (8, RW))
        held = jnp.where((my_row >= first_row) & (my_row < first_row + 256.0), 1.0, 0.0)
        level = levels[e]
        left = (recv[e, :, 0:RW] - level) * held
        right = (recv[e, :, RW : 2 * RW] - level) * held
        weight = held * jnp.broadcast_to(infos[pl.ds(e, 1), :], (8, RW))[:, 2:3]
        mask = cover[pl.ds(e, 1), :]
        acc = [acc[k] + (right if k % 2 else left) * mask[:, k * RW : (k + 1) * RW] for k in range(out_blocks)]
        cnt = [cnt[k] + weight * mask[:, k * RW : (k + 1) * RW] for k in range(out_blocks)]
        return acc, cnt

    zero = [jnp.zeros((8, RW), F32)] * out_blocks
    acc, cnt = lax.fori_loop(0, 64, add_block, (zero, zero))
    for k in range(out_blocks):
        out[0, :, k * RW : (k + 1) * RW] = acc[k] / jnp.maximum(cnt[k], 1.0)


def on_device(
    coadd_image, science, row_offset, col_offset, intersections, visit_weight, basis_index, weights, profiles
):
    any_space = pl.BlockSpec(memory_space=pl.ANY)
    smem = pl.BlockSpec(memory_space=pltpu.SMEM)
    vmem = pl.BlockSpec(memory_space=pltpu.VMEM)
    dma = pltpu.SemaphoreType.DMA
    return pl.pallas_call(
        kernel,
        out_shape=jax.ShapeDtypeStruct((1, 8, 1024), F32),
        in_specs=[any_space, any_space, smem, smem, smem, smem, smem, smem, vmem],
        out_specs=vmem,
        scratch_shapes=[
            pltpu.VMEM((4, 4, 4, 8, 1024), F32),
            pltpu.VMEM((256, 256), F32),
            pltpu.VMEM((16, COLS), F32),
            pltpu.VMEM((COLS, 2 * B * RW), BF16),
            pltpu.VMEM((COLS, 2 * B * RW), BF16),
            pltpu.VMEM((2 * B, 2 * RW, ROWS), BF16),
            pltpu.VMEM((2 * B, 2 * RW, ROWS), BF16),
            pltpu.VMEM((32, 8, 256), F32),
            pltpu.VMEM((64, 8, 256), F32),
            pltpu.VMEM((4, 4, 4, 1, 128), F32),
            pltpu.VMEM((64, 128), F32),
            pltpu.VMEM((64, 1024), F32),
            pltpu.VMEM((64, 128), F32),
            pltpu.VMEM((64, 1, 128), F32),
            pltpu.VMEM((4, 2, 128), F32),
            dma((2,)),
            dma((NPART, 3, 3)),
            dma((NPART, 3, 3)),
            dma((3, 3)),
            dma((3, 3)),
            dma((3,)),
            dma((3,)),
            dma((2,)),
            dma((2,)),
        ],
        compiler_params=pltpu.CompilerParams(
            collective_id=0, has_side_effects=True, vmem_limit_bytes=40 * 1024 * 1024
        ),
        name="difference",
    )(coadd_image, science, row_offset, col_offset, intersections, visit_weight, basis_index, weights, profiles)


def solution(mesh):
    return jax.shard_map(
        on_device,
        mesh=mesh,
        in_specs=(
            P("tile", "epoch", None),
            P("tile", "epoch", None, None),
            P("tile", "epoch"),
            P("tile", "epoch"),
            P("tile", "epoch"),
            P("tile", "epoch"),
            P("tile", "epoch", None, None, None),
            P("tile", "epoch", None, None, None),
            P(),
        ),
        out_specs=P("tile", "epoch", None),
        check_vma=False,
    )
```

```python
import jax
import jax.numpy as jnp
from jax import lax
from jax.experimental import pallas as pl
from jax.experimental.pallas import tpu as pltpu
from jax.sharding import PartitionSpec as P

KW = 31
HALF = 15
RW = 128
B = 3
F32 = jnp.float32
BF16 = jnp.bfloat16
MESH = pl.DeviceIdType.MESH

STRIDES = (16, 4, 1)
PARTS = (
    (0, 384, (1, 2, 0)),
    (384, 384, (1, 0, 2)),
    (768, 256, (2, 0, 1)),
)
NPART = len(PARTS)
ROWS = 384
COLS = 512


def split(value):
    high = value.astype(BF16)
    return high, (value - high.astype(F32)).astype(BF16)


def roll_by(value, amount, axis, limit=None):
    chosen = jnp.broadcast_to(amount, value.shape)
    step = 1
    while step < value.shape[axis]:
        value = jnp.where((chosen & step) != 0, pltpu.roll(value, step, axis), value)
        step *= 2
    return value


def toeplitz(taps, shift, rows):
    width = taps.shape[1]
    base = roll_by(jnp.broadcast_to(taps, (8, width)), shift & 511, 1)
    return pltpu.roll(jnp.broadcast_to(base[0:1, :], (rows, width)), 0, 1, stride=1, stride_axis=0)


def folded_toeplitz(taps, shift, rows, turn):
    row = lax.broadcasted_iota(jnp.int32, (rows, taps.shape[1]), 0)
    return jnp.where(row < turn, toeplitz(taps, shift - turn + rows, rows), toeplitz(taps, shift - turn, rows))


def pick(pieces, start, keep):
    chosen = jnp.broadcast_to(start, pieces[0].shape)
    step = 1
    while step * 2 <= len(pieces) - keep:
        step *= 2
    while step:
        moved = (chosen & step) != 0
        count = min(len(pieces), keep + step - 1)
        pieces = [
            jnp.where(moved, pieces[j + step], pieces[j]) if j + step < len(pieces) else pieces[j]
            for j in range(count)
        ]
        step //= 2
    return pieces


def kernel(
    coadd, science, row_offset, col_offset, intersections, visit_weight, basis_index, weights, profiles,
    out,
    tile, sci, prof, table, hor, ver, sumband, slots, recv, info, infos, cover, held, sums,
    row_s, col_s, int_s, vis_s, bas_s, wei_s,
    local_sem, send_sem, recv_sem, info_send, info_recv, sum_send, sum_recv, a2a_send, a2a_recv,
):
    me_t = lax.axis_index("tile")
    me = lax.axis_index("epoch")
    coord = (me // 16, (me // 4) % 4, me % 4)

    own_copy = pltpu.make_async_copy(coadd.at[0], tile.at[coord[0], coord[1], coord[2]], local_sem.at[0])
    own_copy.start()
    pairs = (
        (row_offset, row_s), (col_offset, col_s), (intersections, int_s), (visit_weight, vis_s),
        (basis_index, bas_s), (weights, wei_s), (profiles, prof),
    )
    small = [pltpu.make_async_copy(src, dst, local_sem.at[2 + i]) for i, (src, dst) in enumerate(pairs)]
    for copy in small:
        copy.start()
    sci_copy = pltpu.make_async_copy(science.at[0, 0], sci, local_sem.at[1])
    sci_copy.start()

    def peer(axis, k):
        here = coord[axis]
        return me + (lax.rem(here + k, 4) - here) * STRIDES[axis]

    barrier = pltpu.get_barrier_semaphore()
    for axis in range(3):
        for k in (1, 2, 3):
            pl.semaphore_signal(barrier, inc=1, device_id={"epoch": peer(axis, k)}, device_id_type=MESH)
    for k in (1, 2, 3):
        pl.semaphore_signal(barrier, inc=1, device_id={"tile": lax.rem(me_t + k, 4)}, device_id_type=MESH)

    table[...] = jnp.zeros_like(table)
    for copy in small:
        copy.wait()
    oy = row_s[0, 0]
    ox = col_s[0, 0]
    flag = int_s[0, 0].astype(F32)
    gain = flag * vis_s[0, 0]
    lane = lax.broadcasted_iota(jnp.int32, (1, 128), 1)
    info[coord[0], coord[1], coord[2]] = jnp.where(
        lane == 0, oy.astype(F32), jnp.where(lane == 1, ox.astype(F32), gain)
    )
    table[:, 0:KW] = prof[...]
    own_copy.wait()
    pl.semaphore_wait(barrier, 12)

    def stage_copies(buffer, cols, order, stage, sends, recvs):
        axis = order[stage]
        where = tuple(slice(None) if a in order[:stage] else coord[a] for a in range(3))
        block = buffer.at[where + ((slice(None),) if cols is None else (slice(None), pl.ds(*cols)))]
        return [
            pltpu.make_async_remote_copy(
                src_ref=block,
                dst_ref=block,
                send_sem=sends.at[k - 1],
                recv_sem=recvs.at[k - 1],
                device_id={"epoch": peer(axis, k)},
                device_id_type=MESH,
            )
            for k in (1, 2, 3)
        ]

    def part_copies(part, stage):
        lo, width, order = PARTS[part]
        return stage_copies(tile, (lo, width), order, stage, send_sem.at[part, stage], recv_sem.at[part, stage])

    def info_copies(stage):
        return stage_copies(info, None, (1, 2, 0), stage, info_send.at[stage], info_recv.at[stage])

    started = []

    def start_stage(stage):
        for part in range(NPART):
            if stage:
                for copy in part_copies(part, stage - 1):
                    copy.wait_recv()
            for copy in part_copies(part, stage):
                copy.start()
                started.append(copy)
        if stage:
            for copy in info_copies(stage - 1):
                copy.wait_recv()
        for copy in info_copies(stage):
            copy.start()
            started.append(copy)

    start_stage(0)

    row_block = jnp.minimum((oy - HALF) >> 6, (512 - ROWS) // 64)
    col_block = jnp.minimum((ox - HALF) >> 7, (1024 - COLS) // 128)
    row_shift = oy - HALF - 64 * row_block
    col_shift = ox - HALF - 128 * col_block
    row_turn = oy & 255
    col_turn = ox & 127

    profile = lax.broadcasted_iota(jnp.int32, (16, COLS), 0)

    def taps_of(index):
        return jnp.sum(jnp.where(profile == index, table[...], 0.0), axis=0, keepdims=True)

    across_sums, down_sums = [], []

    def make_horizontal(s):
        for b in range(B):
            band = folded_toeplitz(taps_of(bas_s[0, 0, s, 0, b]), col_shift + s * RW, RW, col_turn)
            across_sums.append(jnp.sum(band, axis=0, keepdims=True))
            high, low = split(band.T)
            at = pl.ds(b * RW, RW)
            hor[s, 0:COLS, at] = high
            hor[s, COLS : 2 * COLS, at] = low
            hor[s, 2 * COLS : 3 * COLS, at] = high

    def make_vertical(s):
        row = lax.broadcasted_iota(jnp.int32, (2 * RW, 1), 0)
        upper = ((row - row_turn) & 255) < RW
        for b in range(B):
            taps = taps_of(bas_s[0, 0, s, 1, b])
            band = folded_toeplitz(taps, row_shift, 2 * RW, row_turn)
            band = band * jnp.where(upper, wei_s[0, 0, 0, s, b], wei_s[0, 0, 1, s, b])
            band = band[:, 0:ROWS]
            down_sums.append(jnp.sum(band, axis=0, keepdims=True))
            high, low = split(band)
            at = 3 * b * ROWS
            ver[s, :, at : at + ROWS] = high
            ver[s, :, at + ROWS : at + 2 * ROWS] = high
            ver[s, :, at + 2 * ROWS : at + 3 * ROWS] = low

    make_horizontal(0)
    start_stage(1)
    make_horizontal(1)
    make_vertical(0)
    start_stage(2)
    make_vertical(1)

    pad = [jnp.zeros((1, ROWS), F32)] * 2, [jnp.zeros((1, COLS), F32)] * 2
    sumband[...] = lax.dot_general(
        jnp.concatenate(down_sums + pad[0], axis=0),
        jnp.concatenate(across_sums + pad[1], axis=0),
        (((0,), (0,)), ((), ())),
        precision=lax.Precision.HIGHEST,
        preferred_element_type=F32,
    )
    sci_copy.wait()
    science_sum = jnp.sum(sci[...], axis=0, keepdims=True)
    science_sum = science_sum[:, 0:RW] + science_sum[:, RW : 2 * RW]
    for s in range(2):
        at = slice(s * RW, (s + 1) * RW)
        sci[:, at] = roll_by(roll_by(sci[:, at], col_turn, 1), row_turn, 0)

    for part in range(NPART):
        for copy in part_copies(part, 2):
            copy.wait_recv()

    window = pick([tile[:, :, :, :, j * 128 : (j + 1) * 128].reshape(8, 64, 128) for j in range(8)], col_block, 4)
    window = jnp.concatenate([piece.reshape(512, 128) for piece in window], axis=1)
    window = pick([window[j * 64 : (j + 1) * 64] for j in range(8)], row_block, 6)
    window = jnp.concatenate(window, axis=0)
    model_sum = jnp.sum(window * sumband[...], axis=0, keepdims=True)
    total = science_sum
    for j in range(4):
        total = total - model_sum[:, j * 128 : (j + 1) * 128]
    sums[me_t] = jnp.where(
        lax.broadcasted_iota(jnp.int32, (2, RW), 0) == 0, jnp.sum(total) * flag, flag
    )
    sum_copies = [
        pltpu.make_async_remote_copy(
            src_ref=sums.at[me_t],
            dst_ref=sums.at[me_t],
            send_sem=sum_send.at[k - 1],
            recv_sem=sum_recv.at[k - 1],
            device_id={"tile": lax.rem(me_t + k, 4)},
            device_id_type=MESH,
        )
        for k in (1, 2, 3)
    ]
    for copy in sum_copies:
        copy.start()

    win_hi, win_lo = split(window)
    win_all = jnp.concatenate([win_hi, win_hi, win_lo], axis=1)
    level = None
    for s in range(2):
        across = jnp.dot(win_all, hor[s], preferred_element_type=F32)
        stack = []
        for b in range(B):
            x_hi, x_lo = split(across[:, b * RW : (b + 1) * RW])
            stack += [x_hi, x_lo, x_hi]
        model = jnp.dot(ver[s], jnp.concatenate(stack, axis=0), preferred_element_type=F32)
        if s == 0:
            for copy in sum_copies:
                copy.wait_recv()
            both = (sums[0] + sums[1]) + (sums[2] + sums[3])
            level = both[0:1, :] / jnp.maximum(both[1:2, :] * 65536.0, 1.0)
        difference = (sci[:, s * RW : (s + 1) * RW] - model - level) * gain
        slots[s] = difference.reshape(32, 8, RW)

        def send_block(k, carry, s=s):
            target = lax.rem(me + k, 64)
            pltpu.make_async_remote_copy(
                src_ref=slots.at[s, lax.rem(target, 32)],
                dst_ref=recv.at[s, me],
                send_sem=a2a_send.at[s],
                recv_sem=a2a_recv.at[s],
                device_id={"epoch": target},
                device_id_type=MESH,
            ).start()
            return carry

        lax.fori_loop(1, 64, send_block, 0)
        recv[s, me] = slots[s, lax.rem(me, 32)]

    for copy in info_copies(2):
        copy.wait_recv()
    for e in range(64):
        infos[e : e + 1, :] = info[e // 16, (e // 4) % 4, e % 4]
    every = infos[...]
    column = lax.broadcasted_iota(jnp.int32, (64, 1024), 1).astype(F32)
    first = every[:, 1:2]
    for s in range(2):
        least = first + float(s * RW)
        cover[s] = jnp.where((column >= least) & (column < least + float(RW)), 1.0, 0.0)
    row = (me * 8 + lax.broadcasted_iota(jnp.int32, (64, 8), 1)).astype(F32)
    first = every[:, 0:1]
    inside = (row >= first) & (row < first + 256.0)
    count = lax.dot_general(
        jnp.where(inside, every[:, 2:3], 0.0),
        cover[0] + cover[1],
        (((0,), (0,)), ((), ())),
        precision=lax.Precision.HIGHEST,
        preferred_element_type=F32,
    )
    scale = 1.0 / jnp.maximum(count, 1.0)
    my_row = (me * 8 + lax.broadcasted_iota(jnp.int32, (8, RW), 0)).astype(F32)

    def make_held(e, carry):
        first_row = jnp.broadcast_to(infos[pl.ds(e, 1), 0:1], (8, RW))
        held[e] = jnp.where((my_row >= first_row) & (my_row < first_row + 256.0), 1.0, 0.0)
        return carry

    lax.fori_loop(0, 64, make_held, 0, unroll=8)

    for copy in started:
        copy.wait_send()
    for copy in sum_copies:
        copy.wait_send()

    def wait_for(ref, sem):
        pltpu.make_async_copy(ref, ref, sem).wait()

    acc = [jnp.zeros((8, RW), F32)] * 8
    for s in range(2):
        wait_for(recv.at[s, pl.ds(0, 63)], a2a_recv.at[s])

        def add_block(e, acc, s=s):
            block = recv[s, e] * held[e]
            mask = cover[s, pl.ds(e, 1), :]
            return [acc[k] + block * mask[:, k * RW : (k + 1) * RW] for k in range(8)]

        acc = lax.fori_loop(0, 64, add_block, acc, unroll=8)
    for k in range(8):
        out[0, :, k * RW : (k + 1) * RW] = acc[k] * scale[:, k * RW : (k + 1) * RW]
    for s in range(2):
        wait_for(recv.at[s, pl.ds(0, 63)], a2a_send.at[s])


def on_device(
    coadd_image, science, row_offset, col_offset, intersections, visit_weight, basis_index, weights, profiles
):
    any_space = pl.BlockSpec(memory_space=pl.ANY)
    dma = pltpu.SemaphoreType.DMA
    return pl.pallas_call(
        kernel,
        out_shape=jax.ShapeDtypeStruct((1, 8, 1024), F32),
        in_specs=[any_space] * 9,
        out_specs=pl.BlockSpec(memory_space=pltpu.VMEM),
        scratch_shapes=[
            pltpu.VMEM((4, 4, 4, 8, 1024), F32),
            pltpu.VMEM((256, 256), F32),
            pltpu.VMEM((16, KW), F32),
            pltpu.VMEM((16, COLS), F32),
            pltpu.VMEM((2, 3 * COLS, B * RW), BF16),
            pltpu.VMEM((2, 2 * RW, 3 * B * ROWS), BF16),
            pltpu.VMEM((ROWS, COLS), F32),
            pltpu.VMEM((2, 32, 8, RW), F32),
            pltpu.VMEM((2, 64, 8, RW), F32),
            pltpu.VMEM((4, 4, 4, 1, 128), F32),
            pltpu.VMEM((64, 128), F32),
            pltpu.VMEM((2, 64, 1024), F32),
            pltpu.VMEM((64, 8, RW), F32),
            pltpu.VMEM((4, 2, 128), F32),
            pltpu.SMEM((1, 1), jnp.int32),
            pltpu.SMEM((1, 1), jnp.int32),
            pltpu.SMEM((1, 1), jnp.int32),
            pltpu.SMEM((1, 1), F32),
            pltpu.SMEM((1, 1, 2, 2, B), jnp.int32),
            pltpu.SMEM((1, 1, 2, 2, B), F32),
            dma((9,)),
            dma((NPART, 3, 3)),
            dma((NPART, 3, 3)),
            dma((3, 3)),
            dma((3, 3)),
            dma((3,)),
            dma((3,)),
            dma((2,)),
            dma((2,)),
        ],
        compiler_params=pltpu.CompilerParams(
            collective_id=0, has_side_effects=True, vmem_limit_bytes=60 * 1024 * 1024
        ),
        name="difference",
    )(
        coadd_image, science, row_offset, col_offset, intersections, visit_weight,
        jnp.swapaxes(basis_index, 3, 4), weights, profiles,
    )


def solution(mesh):
    return jax.shard_map(
        on_device,
        mesh=mesh,
        in_specs=(
            P("tile", "epoch", None),
            P("tile", "epoch", None, None),
            P("tile", "epoch"),
            P("tile", "epoch"),
            P("tile", "epoch"),
            P("tile", "epoch"),
            P("tile", "epoch", None, None, None),
            P("tile", "epoch", None, None, None),
            P(),
        ),
        out_specs=P("tile", "epoch", None),
        check_vma=False,
    )
```

```python
import jax
import jax.numpy as jnp
from jax import lax
from jax.experimental import pallas as pl
from jax.experimental.pallas import tpu as pltpu
from jax.sharding import PartitionSpec as P

KW = 31
HALF = 15
RW = 128
B = 3
NPROF = 16
PAIRS = NPROF * NPROF
F32 = jnp.float32
BF16 = jnp.bfloat16
MESH = pl.DeviceIdType.MESH


def split(value):
    high = value.astype(BF16)
    return high, (value - high.astype(F32)).astype(BF16)


def roll_by(value, amount, axis):
    chosen = jnp.broadcast_to(amount, value.shape)
    step = 1
    while step < value.shape[axis]:
        value = jnp.where((chosen & step) != 0, pltpu.roll(value, step, axis), value)
        step *= 2
    return value


def wide_dot(a, b):
    high, low = split(a)
    return jnp.dot(
        jnp.concatenate([high, low], axis=1), jnp.concatenate([b, b], axis=0), preferred_element_type=F32
    )


def kernel(
    coadd, science, row_offset, col_offset, intersections, visit_weight, basis_index, weights, profiles,
    out,
    near, sci, prof, table, hor, pairs, pairs_hi, pairs_lo, slots, recv, given, params, masks, model,
    parts, sums,
    row_s, col_s, int_s, vis_s, bas_s, wei_s,
    local_sem, halo_send, halo_recv, sum_send, sum_recv, par_sem, sci_sem, lev_sem,
):
    me_t = lax.axis_index("tile")
    me = lax.axis_index("epoch")

    arrays = (
        (row_offset, row_s), (col_offset, col_s), (intersections, int_s), (visit_weight, vis_s),
        (basis_index, bas_s), (weights, wei_s), (profiles, prof),
    )
    small = [pltpu.make_async_copy(src, dst, local_sem.at[2 + i]) for i, (src, dst) in enumerate(arrays)]
    for copy in small:
        copy.start()
    sci_copy = pltpu.make_async_copy(science.at[0, 0], sci, local_sem.at[1])
    sci_copy.start()
    own_copy = pltpu.make_async_copy(coadd.at[0], near.at[2], local_sem.at[0])
    own_copy.start()

    barrier = pltpu.get_barrier_semaphore()

    def greet(k, carry):
        pl.semaphore_signal(barrier, inc=1, device_id={"epoch": lax.rem(me + k, 64)}, device_id_type=MESH)
        return carry

    lax.fori_loop(1, 64, greet, 0)
    for k in (1, 2, 3):
        pl.semaphore_signal(barrier, inc=1, device_id={"tile": lax.rem(me_t + k, 4)}, device_id_type=MESH)

    for copy in small:
        copy.wait()
    oy = row_s[0, 0]
    ox = col_s[0, 0]
    flag = int_s[0, 0].astype(F32)
    gain = flag * vis_s[0, 0]

    lane = lax.broadcasted_iota(jnp.int32, (2, 128), 1)
    region = lax.broadcasted_iota(jnp.int32, (2, 128), 0)

    def by_region(left, right):
        return jnp.where(region == 0, left, right)

    entries = [oy.astype(F32), by_region(ox.astype(F32), ox.astype(F32) + float(RW)), gain, flag]
    for b in range(B):
        pair = [(bas_s[0, 0, s, 0, b] * NPROF + bas_s[0, 0, s, 1, b]).astype(F32) for s in range(2)]
        entries.append(by_region(*pair))
    for y in range(2):
        for b in range(B):
            entries.append(by_region(wei_s[0, 0, y, 0, b], wei_s[0, 0, y, 1, b]))
    row = jnp.zeros((2, 128), F32)
    for k, entry in enumerate(entries):
        row = jnp.where(lane == k, entry, row)
    given[me] = row

    sci_copy.wait()
    image = sci[...]
    science_sum = jnp.sum(image)
    slots[...] = (roll_by(roll_by(image, ox & 255, 1), oy & 255, 0) * gain).reshape(32, 8, 256)
    own_copy.wait()
    pl.semaphore_wait(barrier, 66)

    def send_params(k, carry):
        pltpu.make_async_remote_copy(
            src_ref=given.at[me],
            dst_ref=given.at[me],
            send_sem=par_sem.at[0],
            recv_sem=par_sem.at[1],
            device_id={"epoch": lax.rem(me + k, 64)},
            device_id_type=MESH,
        ).start()
        return carry

    def send_science(k, carry):
        target = lax.rem(me + k, 64)
        pltpu.make_async_remote_copy(
            src_ref=slots.at[lax.rem(target, 32)],
            dst_ref=recv.at[me],
            send_sem=sci_sem.at[0],
            recv_sem=sci_sem.at[1],
            device_id={"epoch": target},
            device_id_type=MESH,
        ).start()
        return carry

    halo = [
        pltpu.make_async_remote_copy(
            src_ref=near.at[2],
            dst_ref=near.at[2 - d],
            send_sem=halo_send.at[i],
            recv_sem=halo_recv.at[i],
            device_id={"epoch": lax.rem(me + d + 64, 64)},
            device_id_type=MESH,
        )
        for i, d in enumerate((1, -1, 2, -2))
    ]
    for copy in halo:
        copy.start()
    lax.fori_loop(1, 64, send_params, 0)
    lax.fori_loop(1, 64, send_science, 0)
    recv[me] = slots[lax.rem(me, 32)]

    table[...] = jnp.zeros_like(table)
    table[:, 0:KW] = prof[...]
    wide = table[:, 0:128]
    vertical = jnp.concatenate([pltpu.roll(wide, r + 1, 1) for r in range(8)], axis=0)[:, 0:40]
    for q in range(NPROF):
        band = pltpu.roll(
            jnp.broadcast_to(table[q : q + 1, :], (RW, 2 * RW)), 0, 1, stride=1, stride_axis=0
        ).T
        high, low = split(band)
        at = slice(q * RW, (q + 1) * RW)
        hor[0 : 2 * RW, at] = high
        hor[2 * RW : 4 * RW, at] = low
        hor[4 * RW : 6 * RW, at] = high

    for copy in halo:
        copy.wait_recv()
    down = jnp.dot(
        vertical, near[...].reshape(40, 1024), precision=lax.Precision.HIGHEST, preferred_element_type=F32
    )
    down = pltpu.roll(down, HALF, 1)
    high, low = split(down)

    def stacked(value):
        def block(j):
            return value[:, (j % 8) * RW : (j % 8 + 1) * RW]

        return jnp.concatenate(
            [jnp.concatenate([block(j), block(j + 1)], axis=1) for j in range(8)], axis=0
        )

    high, low = stacked(high), stacked(low)
    left = jnp.concatenate([high, high, low], axis=1)
    for step in range(NPROF // 2):
        both = jnp.dot(left, hor[:, step * 256 : (step + 1) * 256], preferred_element_type=F32)
        for half in range(2):
            q = 2 * step + half
            at = slice(q * NPROF, (q + 1) * NPROF)
            for j in range(8):
                cols = slice(j * RW, (j + 1) * RW)
                for r in range(8):
                    top = j * 128 + r * NPROF
                    piece = both[top : top + NPROF, half * RW : (half + 1) * RW]
                    pairs[r, at, cols] = piece
                    high, low = split(piece)
                    pairs_hi[r, at, cols] = high
                    pairs_lo[r, at, cols] = low

    def wait_for(ref, sem):
        pltpu.make_async_copy(ref, ref, sem).wait()

    most = pl.ds(0, 63)
    wait_for(given.at[most], par_sem.at[1])
    for e in range(64):
        params[2 * e : 2 * e + 2, :] = given[e]
    every = params[...]
    across = every.T

    def entry(k):
        return across[k : k + 1, :]

    first = every[:, 1:2]
    column = lax.broadcasted_iota(jnp.int32, (128, 1024), 1).astype(F32)
    cover = jnp.where((column >= first) & (column < first + float(RW)), 1.0, 0.0).astype(BF16)
    column = lax.broadcasted_iota(jnp.int32, (1024, 128), 0).astype(F32)
    cover_t = jnp.where((column >= entry(1)) & (column < entry(1) + float(RW)), 1.0, 0.0).astype(BF16)
    my_row = (me * 8 + lax.broadcasted_iota(jnp.int32, (8, 128), 0)).astype(F32)
    inside = my_row - entry(0)
    upper = jnp.where((inside >= 0.0) & (inside < 128.0), 1.0, 0.0)
    lower = jnp.where((inside >= 128.0) & (inside < 256.0), 1.0, 0.0)

    pair_id = lax.broadcasted_iota(jnp.int32, (PAIRS, 128), 0).astype(F32)
    weight = [jnp.zeros((PAIRS, 128), F32)] * 2
    for b in range(B):
        same = pair_id == entry(4 + b)
        weight = [weight[y] + jnp.where(same, entry(7 + 3 * y + b), 0.0) for y in range(2)]

    def weight_of(r):
        return weight[0] * upper[r : r + 1, :] + weight[1] * lower[r : r + 1, :]

    cover_t2 = jnp.concatenate([cover_t, cover_t], axis=0)
    model_sum = jnp.zeros((1, 128), F32)
    for r in range(8):
        z = jnp.concatenate([pairs_hi[r], pairs_lo[r]], axis=1)
        covered = jnp.dot(z, cover_t2, preferred_element_type=F32)
        model_sum = model_sum + jnp.sum(covered * weight_of(r), axis=0, keepdims=True)
    lane = lax.broadcasted_iota(jnp.int32, (1, 128), 1)
    parts[me] = jnp.where(lane == 2 * me, science_sum, 0.0) - model_sum

    def send_parts(k, carry):
        pltpu.make_async_remote_copy(
            src_ref=parts.at[me],
            dst_ref=parts.at[me],
            send_sem=lev_sem.at[0],
            recv_sem=lev_sem.at[1],
            device_id={"epoch": lax.rem(me + k, 64)},
            device_id_type=MESH,
        ).start()
        return carry

    lax.fori_loop(1, 64, send_parts, 0)

    for r in range(8):
        coef = wide_dot(weight_of(r) * entry(2), cover)
        model[r : r + 1, :] = jnp.sum(pairs[r] * coef, axis=0, keepdims=True)
    count = wide_dot((upper + lower) * entry(2), cover)
    scale = 1.0 / jnp.maximum(count, 1.0)

    column = lax.broadcasted_iota(jnp.int32, (8, 1024), 1).astype(F32)
    rows = (me * 8 + lax.broadcasted_iota(jnp.int32, (8, 1024), 0)).astype(F32)

    def make_mask(e, carry):
        top = jnp.broadcast_to(given[e, 0:1, 0:1], (8, 1024))
        side = jnp.broadcast_to(given[e, 0:1, 1:2], (8, 1024))
        hit = (rows >= top) & (rows < top + 256.0) & (column >= side) & (column < side + 256.0)
        masks[e] = jnp.where(hit, 1.0, 0.0)
        return carry

    lax.fori_loop(0, 64, make_mask, 0, unroll=4)

    wait_for(parts.at[most], lev_sem.at[1])
    total = jnp.sum(parts[...], axis=0)
    even = (lane & 1) == 0
    total = total + jnp.where(even, pltpu.roll(total, 127, 1), pltpu.roll(total, 1, 1))
    sums[me_t] = jnp.concatenate([total * entry(3), entry(3)], axis=0)
    sum_copies = [
        pltpu.make_async_remote_copy(
            src_ref=sums.at[me_t],
            dst_ref=sums.at[me_t],
            send_sem=sum_send.at[k - 1],
            recv_sem=sum_recv.at[k - 1],
            device_id={"tile": lax.rem(me_t + k, 4)},
            device_id_type=MESH,
        )
        for k in (1, 2, 3)
    ]
    for copy in sum_copies:
        copy.start()

    wait_for(recv.at[most], sci_sem.at[1])

    def add_block(e, acc):
        halves = [recv[e, :, 0:RW], recv[e, :, RW : 2 * RW]]
        return [acc[k] + halves[k % 2] * masks[e, :, k * RW : (k + 1) * RW] for k in range(8)]

    acc = lax.fori_loop(0, 64, add_block, [jnp.zeros((8, RW), F32)] * 8, unroll=8)

    for copy in sum_copies:
        copy.wait_recv()
    both = (sums[0] + sums[1]) + (sums[2] + sums[3])
    level = both[0:1, :] / jnp.maximum(both[1:2, :] * 65536.0, 1.0)
    taken = model[...] + wide_dot((upper + lower) * (entry(2) * level), cover)
    for k in range(8):
        at = slice(k * RW, (k + 1) * RW)
        out[0, :, at] = (acc[k] - taken[:, at]) * scale[:, at]

    for copy in halo:
        copy.wait_send()
    for copy in sum_copies:
        copy.wait_send()
    wait_for(given.at[most], par_sem.at[0])
    wait_for(recv.at[most], sci_sem.at[0])
    wait_for(parts.at[most], lev_sem.at[0])


def on_device(
    coadd_image, science, row_offset, col_offset, intersections, visit_weight, basis_index, weights, profiles
):
    any_space = pl.BlockSpec(memory_space=pl.ANY)
    dma = pltpu.SemaphoreType.DMA
    return pl.pallas_call(
        kernel,
        out_shape=jax.ShapeDtypeStruct((1, 8, 1024), F32),
        in_specs=[any_space] * 9,
        out_specs=pl.BlockSpec(memory_space=pltpu.VMEM),
        scratch_shapes=[
            pltpu.VMEM((5, 8, 1024), F32),
            pltpu.VMEM((256, 256), F32),
            pltpu.VMEM((NPROF, KW), F32),
            pltpu.VMEM((NPROF, 2 * RW), F32),
            pltpu.VMEM((6 * RW, NPROF * RW), BF16),
            pltpu.VMEM((8, PAIRS, 1024), F32),
            pltpu.VMEM((8, PAIRS, 1024), BF16),
            pltpu.VMEM((8, PAIRS, 1024), BF16),
            pltpu.VMEM((32, 8, 256), F32),
            pltpu.VMEM((64, 8, 256), F32),
            pltpu.VMEM((64, 2, 128), F32),
            pltpu.VMEM((128, 128), F32),
            pltpu.VMEM((64, 8, 1024), F32),
            pltpu.VMEM((8, 1024), F32),
            pltpu.VMEM((64, 1, 128), F32),
            pltpu.VMEM((4, 2, 128), F32),
            pltpu.SMEM((1, 1), jnp.int32),
            pltpu.SMEM((1, 1), jnp.int32),
            pltpu.SMEM((1, 1), jnp.int32),
            pltpu.SMEM((1, 1), F32),
            pltpu.SMEM((1, 1, 2, 2, B), jnp.int32),
            pltpu.SMEM((1, 1, 2, 2, B), F32),
            dma((9,)),
            dma((4,)),
            dma((4,)),
            dma((3,)),
            dma((3,)),
            dma((2,)),
            dma((2,)),
            dma((2,)),
        ],
        compiler_params=pltpu.CompilerParams(
            collective_id=0, has_side_effects=True, vmem_limit_bytes=60 * 1024 * 1024
        ),
        name="difference",
    )(
        coadd_image, science, row_offset, col_offset, intersections, visit_weight,
        jnp.swapaxes(basis_index, 3, 4), weights, profiles,
    )


def solution(mesh):
    return jax.shard_map(
        on_device,
        mesh=mesh,
        in_specs=(
            P("tile", "epoch", None),
            P("tile", "epoch", None, None),
            P("tile", "epoch"),
            P("tile", "epoch"),
            P("tile", "epoch"),
            P("tile", "epoch"),
            P("tile", "epoch", None, None, None),
            P("tile", "epoch", None, None, None),
            P(),
        ),
        out_specs=P("tile", "epoch", None),
        check_vma=False,
    )
```

```python
import jax
import jax.numpy as jnp
from jax import lax
from jax.experimental import pallas as pl
from jax.experimental.pallas import tpu as pltpu
from jax.sharding import PartitionSpec as P

KW = 31
HALF = 15
RW = 128
B = 3
NPROF = 16
PAIRS = NPROF * NPROF
F32 = jnp.float32
BF16 = jnp.bfloat16
MESH = pl.DeviceIdType.MESH


def split(value):
    high = value.astype(BF16)
    return high, (value - high.astype(F32)).astype(BF16)


def roll_by(value, amount, axis):
    chosen = jnp.broadcast_to(amount, value.shape)
    step = 1
    while step < value.shape[axis]:
        value = jnp.where((chosen & step) != 0, pltpu.roll(value, step, axis), value)
        step *= 2
    return value


def wide_dot(a, b):
    high, low = split(a)
    return jnp.dot(
        jnp.concatenate([high, low], axis=1), jnp.concatenate([b, b], axis=0), preferred_element_type=F32
    )


def kernel(
    coadd, science, row_offset, col_offset, intersections, visit_weight, basis_index, weights, profiles,
    out,
    near, sci, prof, table, hor, pairs, slots, recv, given, params, masks, model,
    parts, sums,
    row_s, col_s, int_s, vis_s, bas_s, wei_s,
    local_sem, halo_send, halo_recv, sum_send, sum_recv, par_sem, sci_sem, lev_sem,
):
    me_t = lax.axis_index("tile")
    me = lax.axis_index("epoch")

    arrays = (
        (row_offset, row_s), (col_offset, col_s), (intersections, int_s), (visit_weight, vis_s),
        (basis_index, bas_s), (weights, wei_s), (profiles, prof),
    )
    small = [pltpu.make_async_copy(src, dst, local_sem.at[2 + i]) for i, (src, dst) in enumerate(arrays)]
    for copy in small:
        copy.start()
    sci_copy = pltpu.make_async_copy(science.at[0, 0], sci, local_sem.at[1])
    sci_copy.start()
    own_copy = pltpu.make_async_copy(coadd.at[0], near.at[2], local_sem.at[0])
    own_copy.start()

    barrier = pltpu.get_barrier_semaphore()

    def greet(k, carry):
        pl.semaphore_signal(barrier, inc=1, device_id={"epoch": lax.rem(me + k, 64)}, device_id_type=MESH)
        return carry

    lax.fori_loop(1, 64, greet, 0)
    for k in (1, 2, 3):
        pl.semaphore_signal(barrier, inc=1, device_id={"tile": lax.rem(me_t + k, 4)}, device_id_type=MESH)

    for copy in small:
        copy.wait()
    oy = row_s[0, 0]
    ox = col_s[0, 0]
    flag = int_s[0, 0].astype(F32)
    gain = flag * vis_s[0, 0]

    lane = lax.broadcasted_iota(jnp.int32, (2, 128), 1)
    region = lax.broadcasted_iota(jnp.int32, (2, 128), 0)

    def by_region(left, right):
        return jnp.where(region == 0, left, right)

    entries = [oy.astype(F32), by_region(ox.astype(F32), ox.astype(F32) + float(RW)), gain, flag]
    for b in range(B):
        pair = [(bas_s[0, 0, s, 0, b] * NPROF + bas_s[0, 0, s, 1, b]).astype(F32) for s in range(2)]
        entries.append(by_region(*pair))
    for y in range(2):
        for b in range(B):
            entries.append(by_region(wei_s[0, 0, y, 0, b], wei_s[0, 0, y, 1, b]))
    for pick in range(2):
        for b in range(B):
            entries.append(by_region(*[bas_s[0, 0, s, pick, b].astype(F32) for s in range(2)]))
    row = jnp.zeros((2, 128), F32)
    for k, entry in enumerate(entries):
        row = jnp.where(lane == k, entry, row)
    given[me] = row

    sci_copy.wait()
    image = sci[...]
    science_sum = jnp.sum(image)
    slots[...] = (roll_by(roll_by(image, ox & 255, 1), oy & 255, 0) * gain).reshape(32, 8, 256)
    own_copy.wait()
    pl.semaphore_wait(barrier, 66)

    def send_params(k, carry):
        pltpu.make_async_remote_copy(
            src_ref=given.at[me],
            dst_ref=given.at[me],
            send_sem=par_sem.at[0],
            recv_sem=par_sem.at[1],
            device_id={"epoch": lax.rem(me + k, 64)},
            device_id_type=MESH,
        ).start()
        return carry

    def send_science(k, carry):
        target = lax.rem(me + k, 64)
        pltpu.make_async_remote_copy(
            src_ref=slots.at[lax.rem(target, 32)],
            dst_ref=recv.at[me],
            send_sem=sci_sem.at[0],
            recv_sem=sci_sem.at[1],
            device_id={"epoch": target},
            device_id_type=MESH,
        ).start()
        return carry

    halo = [
        pltpu.make_async_remote_copy(
            src_ref=near.at[2],
            dst_ref=near.at[2 - d],
            send_sem=halo_send.at[i],
            recv_sem=halo_recv.at[i],
            device_id={"epoch": lax.rem(me + d + 64, 64)},
            device_id_type=MESH,
        )
        for i, d in enumerate((1, -1, 2, -2))
    ]
    for copy in halo:
        copy.start()
    lax.fori_loop(1, 64, send_params, 0)
    lax.fori_loop(1, 64, send_science, 0)
    recv[me] = slots[lax.rem(me, 32)]

    table[...] = jnp.zeros_like(table)
    table[:, 0:KW] = prof[...]
    wide = table[:, 0:128]
    vertical = jnp.concatenate([pltpu.roll(wide, r + 1, 1) for r in range(8)], axis=0)[:, 0:40]
    box = []
    for q in range(NPROF):
        band = pltpu.roll(
            jnp.broadcast_to(table[q : q + 1, :], (RW, 2 * RW)), 0, 1, stride=1, stride_axis=0
        )
        box.append(jnp.sum(band, axis=0, keepdims=True))
        high, low = split(band.T)
        at = slice(q * RW, (q + 1) * RW)
        hor[0 : 2 * RW, at] = high
        hor[2 * RW : 4 * RW, at] = low
        hor[4 * RW : 6 * RW, at] = high

    for copy in halo:
        copy.wait_recv()
    down = jnp.dot(
        vertical, near[...].reshape(40, 1024), precision=lax.Precision.HIGHEST, preferred_element_type=F32
    )
    def wait_for(ref, sem):
        pltpu.make_async_copy(ref, ref, sem).wait()

    most = pl.ds(0, 63)
    wait_for(given.at[most], par_sem.at[1])
    for e in range(64):
        params[2 * e : 2 * e + 2, :] = given[e]
    every = params[...]
    def field(k):
        return every[:, k : k + 1]

    profile = lax.broadcasted_iota(jnp.int32, (128, NPROF), 1).astype(F32)
    chosen = jnp.concatenate([jnp.where(profile == field(13 + b), 1.0, 0.0) for b in range(B)], axis=0)
    boxes = jnp.concatenate([jnp.concatenate(box, axis=0), jnp.zeros((NPROF, RW), F32)], axis=1)
    taken = jnp.dot(chosen, boxes, precision=lax.Precision.HIGHEST, preferred_element_type=F32)
    start = jnp.broadcast_to((field(1) - float(HALF)).astype(jnp.int32), (128, 128))
    start = jnp.concatenate([start] * B, axis=0)
    turn = jnp.concatenate([start] * 3, axis=1)
    for step in (1, 2, 4, 8, 16, 32, 64):
        taken = jnp.where((turn & step) != 0, pltpu.roll(taken, step, 1), taken)
    block = start >> 7
    spread = []
    for j in range(8):
        value = jnp.where(block == j, taken[:, 0:RW], 0.0)
        for d in (1, 2):
            if j >= d:
                value = value + jnp.where(block == j - d, taken[:, d * RW : (d + 1) * RW], 0.0)
        spread.append(value)
    g_hi, g_lo = split(jnp.concatenate(spread, axis=1))
    y_hi, y_lo = split(down)
    caught = lax.dot_general(
        jnp.concatenate([g_hi, g_hi, g_lo], axis=1),
        jnp.concatenate([y_hi, y_lo, y_hi], axis=1),
        (((1,), (1,)), ((), ())),
        preferred_element_type=F32,
    )
    place = lax.broadcasted_iota(jnp.int32, (128, 128), 1)
    offset = (me * 8 + (place >> 4)).astype(F32) - field(0)
    place = (place & 15).astype(F32)
    upper = (offset >= 0.0) & (offset < 128.0)
    lower = (offset >= 128.0) & (offset < 256.0)
    sum_of = jnp.zeros((128, 128), F32)
    for b in range(B):
        part = jnp.where(upper, field(7 + b), 0.0) + jnp.where(lower, field(10 + b), 0.0)
        sum_of = sum_of + jnp.where(place == field(16 + b), part, 0.0) * caught[b * 128 : (b + 1) * 128]
    model_sum = jnp.sum(sum_of.T, axis=0, keepdims=True)
    lane = lax.broadcasted_iota(jnp.int32, (1, 128), 1)
    parts[me] = jnp.where(lane == 2 * me, science_sum, 0.0) - model_sum

    def send_parts(k, carry):
        pltpu.make_async_remote_copy(
            src_ref=parts.at[me],
            dst_ref=parts.at[me],
            send_sem=lev_sem.at[0],
            recv_sem=lev_sem.at[1],
            device_id={"epoch": lax.rem(me + k, 64)},
            device_id_type=MESH,
        ).start()
        return carry

    lax.fori_loop(1, 64, send_parts, 0)

    down = pltpu.roll(down, HALF, 1)
    high, low = split(down)

    def stacked(value):
        def block(j):
            return value[:, (j % 8) * RW : (j % 8 + 1) * RW]

        return jnp.concatenate(
            [jnp.concatenate([block(j), block(j + 1)], axis=1) for j in range(8)], axis=0
        )

    high, low = stacked(high), stacked(low)
    left = jnp.concatenate([high, high, low], axis=1)
    for step in range(NPROF // 2):
        both = jnp.dot(left, hor[:, step * 256 : (step + 1) * 256], preferred_element_type=F32)
        for half in range(2):
            q = 2 * step + half
            at = slice(q * NPROF, (q + 1) * NPROF)
            for j in range(8):
                cols = slice(j * RW, (j + 1) * RW)
                for r in range(8):
                    top = j * 128 + r * NPROF
                    pairs[r, at, cols] = both[top : top + NPROF, half * RW : (half + 1) * RW]

    across = every.T

    def entry(k):
        return across[k : k + 1, :]

    first = every[:, 1:2]
    column = lax.broadcasted_iota(jnp.int32, (128, 1024), 1).astype(F32)
    cover = jnp.where((column >= first) & (column < first + float(RW)), 1.0, 0.0).astype(BF16)
    my_row = (me * 8 + lax.broadcasted_iota(jnp.int32, (8, 128), 0)).astype(F32)
    inside = my_row - entry(0)
    upper = jnp.where((inside >= 0.0) & (inside < 128.0), 1.0, 0.0)
    lower = jnp.where((inside >= 128.0) & (inside < 256.0), 1.0, 0.0)

    pair_id = lax.broadcasted_iota(jnp.int32, (PAIRS, 128), 0).astype(F32)
    weight = [jnp.zeros((PAIRS, 128), F32)] * 2
    for b in range(B):
        same = pair_id == entry(4 + b)
        weight = [weight[y] + jnp.where(same, entry(7 + 3 * y + b), 0.0) for y in range(2)]

    def weight_of(r):
        return weight[0] * upper[r : r + 1, :] + weight[1] * lower[r : r + 1, :]

    column = lax.broadcasted_iota(jnp.int32, (8, 1024), 1).astype(F32)
    rows = (me * 8 + lax.broadcasted_iota(jnp.int32, (8, 1024), 0)).astype(F32)

    def make_mask(e, carry):
        top = jnp.broadcast_to(given[e, 0:1, 0:1], (8, 1024))
        side = jnp.broadcast_to(given[e, 0:1, 1:2], (8, 1024))
        hit = (rows >= top) & (rows < top + 256.0) & (column >= side) & (column < side + 256.0)
        masks[e] = jnp.where(hit, 1.0, 0.0)
        return carry

    lax.fori_loop(0, 64, make_mask, 0, unroll=4)

    wait_for(parts.at[most], lev_sem.at[1])
    total = jnp.sum(parts[...], axis=0)
    even = (lane & 1) == 0
    total = total + jnp.where(even, pltpu.roll(total, 127, 1), pltpu.roll(total, 1, 1))
    sums[me_t] = jnp.concatenate([total * entry(3), entry(3)], axis=0)
    sum_copies = [
        pltpu.make_async_remote_copy(
            src_ref=sums.at[me_t],
            dst_ref=sums.at[me_t],
            send_sem=sum_send.at[k - 1],
            recv_sem=sum_recv.at[k - 1],
            device_id={"tile": lax.rem(me_t + k, 4)},
            device_id_type=MESH,
        )
        for k in (1, 2, 3)
    ]
    for copy in sum_copies:
        copy.start()

    for r in range(8):
        coef = wide_dot(weight_of(r) * entry(2), cover)
        model[r : r + 1, :] = jnp.sum(pairs[r] * coef, axis=0, keepdims=True)
    count = wide_dot((upper + lower) * entry(2), cover)
    scale = 1.0 / jnp.maximum(count, 1.0)

    wait_for(recv.at[most], sci_sem.at[1])

    def add_block(e, acc):
        halves = [recv[e, :, 0:RW], recv[e, :, RW : 2 * RW]]
        return [acc[k] + halves[k % 2] * masks[e, :, k * RW : (k + 1) * RW] for k in range(8)]

    acc = lax.fori_loop(0, 64, add_block, [jnp.zeros((8, RW), F32)] * 8, unroll=8)

    for copy in sum_copies:
        copy.wait_recv()
    both = (sums[0] + sums[1]) + (sums[2] + sums[3])
    level = both[0:1, :] / jnp.maximum(both[1:2, :] * 65536.0, 1.0)
    taken = model[...] + wide_dot((upper + lower) * (entry(2) * level), cover)
    for k in range(8):
        at = slice(k * RW, (k + 1) * RW)
        out[0, :, at] = (acc[k] - taken[:, at]) * scale[:, at]

    for copy in halo:
        copy.wait_send()
    for copy in sum_copies:
        copy.wait_send()
    wait_for(given.at[most], par_sem.at[0])
    wait_for(recv.at[most], sci_sem.at[0])
    wait_for(parts.at[most], lev_sem.at[0])


def on_device(
    coadd_image, science, row_offset, col_offset, intersections, visit_weight, basis_index, weights, profiles
):
    any_space = pl.BlockSpec(memory_space=pl.ANY)
    dma = pltpu.SemaphoreType.DMA
    return pl.pallas_call(
        kernel,
        out_shape=jax.ShapeDtypeStruct((1, 8, 1024), F32),
        in_specs=[any_space] * 9,
        out_specs=pl.BlockSpec(memory_space=pltpu.VMEM),
        scratch_shapes=[
            pltpu.VMEM((5, 8, 1024), F32),
            pltpu.VMEM((256, 256), F32),
            pltpu.VMEM((NPROF, KW), F32),
            pltpu.VMEM((NPROF, 2 * RW), F32),
            pltpu.VMEM((6 * RW, NPROF * RW), BF16),
            pltpu.VMEM((8, PAIRS, 1024), F32),
            pltpu.VMEM((32, 8, 256), F32),
            pltpu.VMEM((64, 8, 256), F32),
            pltpu.VMEM((64, 2, 128), F32),
            pltpu.VMEM((128, 128), F32),
            pltpu.VMEM((64, 8, 1024), F32),
            pltpu.VMEM((8, 1024), F32),
            pltpu.VMEM((64, 1, 128), F32),
            pltpu.VMEM((4, 2, 128), F32),
            pltpu.SMEM((1, 1), jnp.int32),
            pltpu.SMEM((1, 1), jnp.int32),
            pltpu.SMEM((1, 1), jnp.int32),
            pltpu.SMEM((1, 1), F32),
            pltpu.SMEM((1, 1, 2, 2, B), jnp.int32),
            pltpu.SMEM((1, 1, 2, 2, B), F32),
            dma((9,)),
            dma((4,)),
            dma((4,)),
            dma((3,)),
            dma((3,)),
            dma((2,)),
            dma((2,)),
            dma((2,)),
        ],
        compiler_params=pltpu.CompilerParams(
            collective_id=0, has_side_effects=True, vmem_limit_bytes=60 * 1024 * 1024
        ),
        name="difference",
    )(
        coadd_image, science, row_offset, col_offset, intersections, visit_weight,
        jnp.swapaxes(basis_index, 3, 4), weights, profiles,
    )


def solution(mesh):
    return jax.shard_map(
        on_device,
        mesh=mesh,
        in_specs=(
            P("tile", "epoch", None),
            P("tile", "epoch", None, None),
            P("tile", "epoch"),
            P("tile", "epoch"),
            P("tile", "epoch"),
            P("tile", "epoch"),
            P("tile", "epoch", None, None, None),
            P("tile", "epoch", None, None, None),
            P(),
        ),
        out_specs=P("tile", "epoch", None),
        check_vma=False,
    )
```

```python
import jax
import jax.numpy as jnp
from jax import lax
from jax.experimental import pallas as pl
from jax.experimental.pallas import tpu as pltpu
from jax.sharding import PartitionSpec as P

KW = 31
HALF = 15
RW = 128
B = 3
NPROF = 16
PAIRS = NPROF * NPROF
EARLY = 4
F32 = jnp.float32
BF16 = jnp.bfloat16
MESH = pl.DeviceIdType.MESH


def split(value):
    high = value.astype(BF16)
    return high, (value - high.astype(F32)).astype(BF16)


def roll_by(value, amount, axis):
    chosen = jnp.broadcast_to(amount, value.shape)
    step = 1
    while step < value.shape[axis]:
        value = jnp.where((chosen & step) != 0, pltpu.roll(value, step, axis), value)
        step *= 2
    return value


def wide_dot(a, b):
    high, low = split(a)
    return jnp.dot(
        jnp.concatenate([high, low], axis=1), jnp.concatenate([b, b], axis=0), preferred_element_type=F32
    )


def kernel(
    coadd, science, row_offset, col_offset, intersections, visit_weight, basis_index, weights, profiles,
    out,
    near, sci, prof, table, hor, pairs, slots, recv, given, params, masks, model,
    parts, sums,
    row_s, col_s, int_s, vis_s, bas_s, wei_s,
    local_sem, halo_send, halo_recv, sum_send, sum_recv, par_sem, sci_sem, lev_sem,
):
    me_t = lax.axis_index("tile")
    me = lax.axis_index("epoch")

    arrays = (
        (row_offset, row_s), (col_offset, col_s), (intersections, int_s), (visit_weight, vis_s),
        (basis_index, bas_s), (weights, wei_s), (profiles, prof),
    )
    small = [pltpu.make_async_copy(src, dst, local_sem.at[2 + i]) for i, (src, dst) in enumerate(arrays)]
    for copy in small:
        copy.start()
    sci_copy = pltpu.make_async_copy(science.at[0, 0], sci, local_sem.at[1])
    sci_copy.start()
    own_copy = pltpu.make_async_copy(coadd.at[0], near.at[2], local_sem.at[0])
    own_copy.start()

    barrier = pltpu.get_barrier_semaphore()

    def greet(k, carry):
        pl.semaphore_signal(barrier, inc=1, device_id={"epoch": ((me + k) & 63)}, device_id_type=MESH)
        return carry

    lax.fori_loop(1, 64, greet, 0, unroll=7)
    for k in (1, 2, 3):
        pl.semaphore_signal(barrier, inc=1, device_id={"tile": ((me_t + k) & 3)}, device_id_type=MESH)

    for copy in small:
        copy.wait()
    oy = row_s[0, 0]
    ox = col_s[0, 0]
    flag = int_s[0, 0].astype(F32)
    gain = flag * vis_s[0, 0]

    lane = lax.broadcasted_iota(jnp.int32, (2, 128), 1)
    region = lax.broadcasted_iota(jnp.int32, (2, 128), 0)

    def by_region(left, right):
        return jnp.where(region == 0, left, right)

    entries = [oy.astype(F32), by_region(ox.astype(F32), ox.astype(F32) + float(RW)), gain, flag]
    for b in range(B):
        pair = [(bas_s[0, 0, s, 0, b] * NPROF + bas_s[0, 0, s, 1, b]).astype(F32) for s in range(2)]
        entries.append(by_region(*pair))
    for y in range(2):
        for b in range(B):
            entries.append(by_region(wei_s[0, 0, y, 0, b], wei_s[0, 0, y, 1, b]))
    for pick in range(2):
        for b in range(B):
            entries.append(by_region(*[bas_s[0, 0, s, pick, b].astype(F32) for s in range(2)]))
    row = jnp.zeros((2, 128), F32)
    for k, entry in enumerate(entries):
        row = jnp.where(lane == k, entry, row)
    given[me] = row

    sci_copy.wait()
    image = sci[...]
    science_sum = jnp.sum(image)
    slots[...] = (roll_by(roll_by(image, ox & 255, 1), oy & 255, 0) * gain).reshape(32, 8, 256)
    own_copy.wait()
    pl.semaphore_wait(barrier, 66)

    def send_params(k, carry):
        pltpu.make_async_remote_copy(
            src_ref=given.at[me],
            dst_ref=given.at[me],
            send_sem=par_sem.at[0],
            recv_sem=par_sem.at[1],
            device_id={"epoch": ((me + k) & 63)},
            device_id_type=MESH,
        ).start()
        return carry

    def send_science(k, carry):
        target = ((me + k) & 63)
        pltpu.make_async_remote_copy(
            src_ref=slots.at[(target & 31)],
            dst_ref=recv.at[me],
            send_sem=sci_sem.at[0],
            recv_sem=sci_sem.at[1],
            device_id={"epoch": target},
            device_id_type=MESH,
        ).start()
        return carry

    halo = [
        pltpu.make_async_remote_copy(
            src_ref=near.at[2],
            dst_ref=near.at[2 - d],
            send_sem=halo_send.at[i],
            recv_sem=halo_recv.at[i],
            device_id={"epoch": ((me + d) & 63)},
            device_id_type=MESH,
        )
        for i, d in enumerate((1, -1, 2, -2))
    ]
    for copy in halo:
        copy.start()
    lax.fori_loop(1, 64, send_params, 0, unroll=7)
    lax.fori_loop(1, 64, send_science, 0, unroll=7)
    recv[me] = slots[(me & 31)]

    table[...] = jnp.zeros_like(table)
    table[:, 0:KW] = prof[...]
    wide = table[:, 0:128]
    vertical = jnp.concatenate([pltpu.roll(wide, r + 1, 1) for r in range(8)], axis=0)[:, 0:40]
    box = []
    for q in range(NPROF):
        band = pltpu.roll(
            jnp.broadcast_to(table[q : q + 1, :], (RW, 2 * RW)), 0, 1, stride=1, stride_axis=0
        )
        box.append(jnp.sum(band, axis=0, keepdims=True))
        high, low = split(band.T)
        at = slice(q * RW, (q + 1) * RW)
        hor[0 : 2 * RW, at] = high
        hor[2 * RW : 4 * RW, at] = low
        hor[4 * RW : 6 * RW, at] = high

    for copy in halo:
        copy.wait_recv()
    down = jnp.dot(
        vertical, near[...].reshape(40, 1024), precision=lax.Precision.HIGHEST, preferred_element_type=F32
    )
    y_hi, y_lo = split(down)
    y_all = jnp.concatenate([y_hi, y_lo, y_hi], axis=1)
    def wait_for(ref, sem):
        pltpu.make_async_copy(ref, ref, sem).wait()

    most = pl.ds(0, 63)
    wait_for(given.at[most], par_sem.at[1])
    for e in range(64):
        params[2 * e : 2 * e + 2, :] = given[e]
    every = params[...]
    def field(k):
        return every[:, k : k + 1]

    profile = lax.broadcasted_iota(jnp.int32, (128, NPROF), 1).astype(F32)
    chosen = jnp.concatenate([jnp.where(profile == field(13 + b), 1.0, 0.0) for b in range(B)], axis=0)
    boxes = jnp.concatenate([jnp.concatenate(box, axis=0), jnp.zeros((NPROF, RW), F32)], axis=1)
    taken = jnp.dot(chosen, boxes, precision=lax.Precision.HIGHEST, preferred_element_type=F32)
    start = jnp.broadcast_to((field(1) - float(HALF)).astype(jnp.int32), (128, 128))
    start = jnp.concatenate([start] * B, axis=0)
    turn = jnp.concatenate([start] * 3, axis=1)
    for step in (1, 2, 4, 8, 16, 32, 64):
        taken = jnp.where((turn & step) != 0, pltpu.roll(taken, step, 1), taken)
    block = start >> 7
    spread = []
    for j in range(8):
        value = jnp.where(block == j, taken[:, 0:RW], 0.0)
        for d in (1, 2):
            if j >= d:
                value = value + jnp.where(block == j - d, taken[:, d * RW : (d + 1) * RW], 0.0)
        spread.append(value)
    g_hi, g_lo = split(jnp.concatenate(spread, axis=1))
    caught = lax.dot_general(
        jnp.concatenate([g_hi, g_hi, g_lo], axis=1),
        y_all,
        (((1,), (1,)), ((), ())),
        preferred_element_type=F32,
    )
    place = lax.broadcasted_iota(jnp.int32, (128, 128), 1)
    offset = (me * 8 + (place >> 4)).astype(F32) - field(0)
    place = (place & 15).astype(F32)
    upper = (offset >= 0.0) & (offset < 128.0)
    lower = (offset >= 128.0) & (offset < 256.0)
    sum_of = jnp.zeros((128, 128), F32)
    for b in range(B):
        part = jnp.where(upper, field(7 + b), 0.0) + jnp.where(lower, field(10 + b), 0.0)
        sum_of = sum_of + jnp.where(place == field(16 + b), part, 0.0) * caught[b * 128 : (b + 1) * 128]
    model_sum = jnp.sum(sum_of.T, axis=0, keepdims=True)
    lane = lax.broadcasted_iota(jnp.int32, (1, 128), 1)
    parts[me] = jnp.where(lane == 2 * me, science_sum, 0.0) - model_sum

    def send_parts(k, carry):
        pltpu.make_async_remote_copy(
            src_ref=parts.at[me],
            dst_ref=parts.at[me],
            send_sem=lev_sem.at[0],
            recv_sem=lev_sem.at[1],
            device_id={"epoch": ((me + k) & 63)},
            device_id_type=MESH,
        ).start()
        return carry

    lax.fori_loop(1, 64, send_parts, 0, unroll=7)

    high, low = split(pltpu.roll(down, HALF, 1))

    def stacked(value):
        def block(j):
            return value[:, (j % 8) * RW : (j % 8 + 1) * RW]

        return jnp.concatenate(
            [jnp.concatenate([block(j), block(j + 1)], axis=1) for j in range(8)], axis=0
        )

    high, low = stacked(high), stacked(low)
    left = jnp.concatenate([high, high, low], axis=1)

    def make_pairs(step):
        both = jnp.dot(left, hor[:, step * 256 : (step + 1) * 256], preferred_element_type=F32)
        for half in range(2):
            q = 2 * step + half
            at = slice(q * NPROF, (q + 1) * NPROF)
            for j in range(8):
                cols = slice(j * RW, (j + 1) * RW)
                for r in range(8):
                    top = j * 128 + r * NPROF
                    pairs[r, at, cols] = both[top : top + NPROF, half * RW : (half + 1) * RW]

    for step in range(EARLY):
        make_pairs(step)

    across = every.T

    def entry(k):
        return across[k : k + 1, :]

    wait_for(parts.at[most], lev_sem.at[1])
    total = jnp.sum(parts[...], axis=0)
    even = (lane & 1) == 0
    total = total + jnp.where(even, pltpu.roll(total, 127, 1), pltpu.roll(total, 1, 1))
    sums[me_t] = jnp.concatenate([total * entry(3), entry(3)], axis=0)
    sum_copies = [
        pltpu.make_async_remote_copy(
            src_ref=sums.at[me_t],
            dst_ref=sums.at[me_t],
            send_sem=sum_send.at[k - 1],
            recv_sem=sum_recv.at[k - 1],
            device_id={"tile": ((me_t + k) & 3)},
            device_id_type=MESH,
        )
        for k in (1, 2, 3)
    ]
    for copy in sum_copies:
        copy.start()

    first = every[:, 1:2]
    column = lax.broadcasted_iota(jnp.int32, (128, 1024), 1).astype(F32)
    cover = jnp.where((column >= first) & (column < first + float(RW)), 1.0, 0.0).astype(BF16)
    my_row = (me * 8 + lax.broadcasted_iota(jnp.int32, (8, 128), 0)).astype(F32)
    inside = my_row - entry(0)
    upper = jnp.where((inside >= 0.0) & (inside < 128.0), 1.0, 0.0)
    lower = jnp.where((inside >= 128.0) & (inside < 256.0), 1.0, 0.0)

    pair_id = lax.broadcasted_iota(jnp.int32, (PAIRS, 128), 0).astype(F32)
    weight = [jnp.zeros((PAIRS, 128), F32)] * 2
    for b in range(B):
        same = pair_id == entry(4 + b)
        weight = [weight[y] + jnp.where(same, entry(7 + 3 * y + b), 0.0) for y in range(2)]

    def weight_of(r):
        return weight[0] * upper[r : r + 1, :] + weight[1] * lower[r : r + 1, :]

    for step in range(EARLY, NPROF // 2):
        make_pairs(step)
    column = lax.broadcasted_iota(jnp.int32, (8, 1024), 1).astype(F32)
    rows = (me * 8 + lax.broadcasted_iota(jnp.int32, (8, 1024), 0)).astype(F32)

    def make_mask(e, carry):
        top = jnp.broadcast_to(given[e, 0:1, 0:1], (8, 1024))
        side = jnp.broadcast_to(given[e, 0:1, 1:2], (8, 1024))
        hit = (rows >= top) & (rows < top + 256.0) & (column >= side) & (column < side + 256.0)
        masks[e] = jnp.where(hit, 1.0, 0.0)
        return carry

    lax.fori_loop(0, 64, make_mask, 0, unroll=4)

    for r in range(8):
        coef = wide_dot(weight_of(r) * entry(2), cover)
        model[r : r + 1, :] = jnp.sum(pairs[r] * coef, axis=0, keepdims=True)
    count = wide_dot((upper + lower) * entry(2), cover)
    scale = 1.0 / jnp.maximum(count, 1.0)

    wait_for(recv.at[most], sci_sem.at[1])

    def add_block(e, acc):
        halves = [recv[e, :, 0:RW], recv[e, :, RW : 2 * RW]]
        return [acc[k] + halves[k % 2] * masks[e, :, k * RW : (k + 1) * RW] for k in range(8)]

    acc = lax.fori_loop(0, 64, add_block, [jnp.zeros((8, RW), F32)] * 8, unroll=8)

    for copy in sum_copies:
        copy.wait_recv()
    both = (sums[0] + sums[1]) + (sums[2] + sums[3])
    level = both[0:1, :] / jnp.maximum(both[1:2, :] * 65536.0, 1.0)
    taken = model[...] + wide_dot((upper + lower) * (entry(2) * level), cover)
    for k in range(8):
        at = slice(k * RW, (k + 1) * RW)
        out[0, :, at] = (acc[k] - taken[:, at]) * scale[:, at]

    for copy in halo:
        copy.wait_send()
    for copy in sum_copies:
        copy.wait_send()
    wait_for(given.at[most], par_sem.at[0])
    wait_for(recv.at[most], sci_sem.at[0])
    wait_for(parts.at[most], lev_sem.at[0])


def on_device(
    coadd_image, science, row_offset, col_offset, intersections, visit_weight, basis_index, weights, profiles
):
    any_space = pl.BlockSpec(memory_space=pl.ANY)
    dma = pltpu.SemaphoreType.DMA
    return pl.pallas_call(
        kernel,
        out_shape=jax.ShapeDtypeStruct((1, 8, 1024), F32),
        in_specs=[any_space] * 9,
        out_specs=pl.BlockSpec(memory_space=pltpu.VMEM),
        scratch_shapes=[
            pltpu.VMEM((5, 8, 1024), F32),
            pltpu.VMEM((256, 256), F32),
            pltpu.VMEM((NPROF, KW), F32),
            pltpu.VMEM((NPROF, 2 * RW), F32),
            pltpu.VMEM((6 * RW, NPROF * RW), BF16),
            pltpu.VMEM((8, PAIRS, 1024), F32),
            pltpu.VMEM((32, 8, 256), F32),
            pltpu.VMEM((64, 8, 256), F32),
            pltpu.VMEM((64, 2, 128), F32),
            pltpu.VMEM((128, 128), F32),
            pltpu.VMEM((64, 8, 1024), F32),
            pltpu.VMEM((8, 1024), F32),
            pltpu.VMEM((64, 1, 128), F32),
            pltpu.VMEM((4, 2, 128), F32),
            pltpu.SMEM((1, 1), jnp.int32),
            pltpu.SMEM((1, 1), jnp.int32),
            pltpu.SMEM((1, 1), jnp.int32),
            pltpu.SMEM((1, 1), F32),
            pltpu.SMEM((1, 1, 2, 2, B), jnp.int32),
            pltpu.SMEM((1, 1, 2, 2, B), F32),
            dma((9,)),
            dma((4,)),
            dma((4,)),
            dma((3,)),
            dma((3,)),
            dma((2,)),
            dma((2,)),
            dma((2,)),
        ],
        compiler_params=pltpu.CompilerParams(
            collective_id=0, has_side_effects=True, vmem_limit_bytes=60 * 1024 * 1024
        ),
        name="difference",
    )(
        coadd_image, science, row_offset, col_offset, intersections, visit_weight,
        jnp.swapaxes(basis_index, 3, 4), weights, profiles,
    )


def solution(mesh):
    return jax.shard_map(
        on_device,
        mesh=mesh,
        in_specs=(
            P("tile", "epoch", None),
            P("tile", "epoch", None, None),
            P("tile", "epoch"),
            P("tile", "epoch"),
            P("tile", "epoch"),
            P("tile", "epoch"),
            P("tile", "epoch", None, None, None),
            P("tile", "epoch", None, None, None),
            P(),
        ),
        out_specs=P("tile", "epoch", None),
        check_vma=False,
    )
```

```python
import jax
import jax.numpy as jnp
from jax import lax
from jax.experimental import pallas as pl
from jax.experimental.pallas import tpu as pltpu
from jax.sharding import PartitionSpec as P

KW = 31
HALF = 15
RW = 128
B = 3
NPROF = 16
PAIRS = NPROF * NPROF
FIRST = 29
EARLY = 4
F32 = jnp.float32
BF16 = jnp.bfloat16
MESH = pl.DeviceIdType.MESH


def split(value):
    high = value.astype(BF16)
    return high, (value - high.astype(F32)).astype(BF16)


def roll_by(value, amount, axis):
    chosen = jnp.broadcast_to(amount, value.shape)
    step = 1
    while step < value.shape[axis]:
        value = jnp.where((chosen & step) != 0, pltpu.roll(value, step, axis), value)
        step *= 2
    return value


def wide_dot(a, b):
    high, low = split(a)
    return jnp.dot(
        jnp.concatenate([high, low], axis=1), jnp.concatenate([b, b], axis=0), preferred_element_type=F32
    )


def kernel(
    coadd, science, row_offset, col_offset, intersections, visit_weight, basis_index, weights, profiles,
    out,
    near, sci, prof, table, hor, pairs, slots, recv, given, params, masks, model,
    parts, sums,
    row_s, col_s, int_s, vis_s, bas_s, wei_s,
    local_sem, halo_send, halo_recv, sum_send, sum_recv, par_sem, sci_sem, lev_sem,
):
    me_t = lax.axis_index("tile")
    me = lax.axis_index("epoch")

    arrays = (
        (row_offset, row_s), (col_offset, col_s), (intersections, int_s), (visit_weight, vis_s),
        (basis_index, bas_s), (weights, wei_s), (profiles, prof),
    )
    small = [pltpu.make_async_copy(src, dst, local_sem.at[2 + i]) for i, (src, dst) in enumerate(arrays)]
    for copy in small:
        copy.start()
    sci_copy = pltpu.make_async_copy(science.at[0, 0], sci, local_sem.at[1])
    sci_copy.start()
    own_copy = pltpu.make_async_copy(coadd.at[0], near.at[2], local_sem.at[0])
    own_copy.start()

    barrier = pltpu.get_barrier_semaphore()

    def greet(k, carry):
        pl.semaphore_signal(barrier, inc=1, device_id={"epoch": (me + k) & 63}, device_id_type=MESH)
        return carry

    lax.fori_loop(1, 64, greet, 0, unroll=7)
    for k in (1, 2, 3):
        pl.semaphore_signal(barrier, inc=1, device_id={"tile": (me_t + k) & 3}, device_id_type=MESH)

    for copy in small:
        copy.wait()
    oy = row_s[0, 0]
    ox = col_s[0, 0]
    flag = int_s[0, 0].astype(F32)
    gain = flag * vis_s[0, 0]

    lane = lax.broadcasted_iota(jnp.int32, (2, 128), 1)
    region = lax.broadcasted_iota(jnp.int32, (2, 128), 0)

    def by_region(left, right):
        return jnp.where(region == 0, left, right)

    entries = [oy.astype(F32), by_region(ox.astype(F32), ox.astype(F32) + float(RW)), gain, flag]
    for b in range(B):
        pair = [(bas_s[0, 0, s, 0, b] * NPROF + bas_s[0, 0, s, 1, b]).astype(F32) for s in range(2)]
        entries.append(by_region(*pair))
    for y in range(2):
        for b in range(B):
            entries.append(by_region(wei_s[0, 0, y, 0, b], wei_s[0, 0, y, 1, b]))
    for pick in range(2):
        for b in range(B):
            entries.append(by_region(*[bas_s[0, 0, s, pick, b].astype(F32) for s in range(2)]))
    row = jnp.zeros((2, 128), F32)
    for k, entry in enumerate(entries):
        row = jnp.where(lane == k, entry, row)
    given[me] = row

    sci_copy.wait()
    image = sci[...]
    science_sum = jnp.sum(image)
    slots[...] = (roll_by(roll_by(image, ox & 255, 1), oy & 255, 0) * gain).reshape(32, 8, 256)
    own_copy.wait()
    pl.semaphore_wait(barrier, 66)

    def send_params(k, carry):
        pltpu.make_async_remote_copy(
            src_ref=given.at[me],
            dst_ref=given.at[me],
            send_sem=par_sem.at[0],
            recv_sem=par_sem.at[1],
            device_id={"epoch": (me + k) & 63},
            device_id_type=MESH,
        ).start()
        return carry

    def send_science(k, carry):
        target = (me + 37 * k) & 63
        pltpu.make_async_remote_copy(
            src_ref=slots.at[(target & 31)],
            dst_ref=recv.at[me],
            send_sem=sci_sem.at[0],
            recv_sem=sci_sem.at[1],
            device_id={"epoch": target},
            device_id_type=MESH,
        ).start()
        return carry

    halo = [
        pltpu.make_async_remote_copy(
            src_ref=near.at[2],
            dst_ref=near.at[2 - d],
            send_sem=halo_send.at[i],
            recv_sem=halo_recv.at[i],
            device_id={"epoch": (me + d) & 63},
            device_id_type=MESH,
        )
        for i, d in enumerate((1, -1, 2, -2))
    ]
    for copy in halo:
        copy.start()
    lax.fori_loop(1, 64, send_params, 0, unroll=7)
    lax.fori_loop(1, FIRST, send_science, 0, unroll=7)
    recv[me] = slots[(me & 31)]

    table[...] = jnp.zeros_like(table)
    table[:, 0:KW] = prof[...]
    wide = table[:, 0:128]
    vertical = jnp.concatenate([pltpu.roll(wide, r + 1, 1) for r in range(8)], axis=0)[:, 0:40]
    box = []
    for q in range(NPROF):
        band = pltpu.roll(
            jnp.broadcast_to(table[q : q + 1, :], (RW, 2 * RW)), 0, 1, stride=1, stride_axis=0
        )
        box.append(jnp.sum(band, axis=0, keepdims=True))
        high, low = split(band.T)
        at = slice(q * RW, (q + 1) * RW)
        hor[0 : 2 * RW, at] = high
        hor[2 * RW : 4 * RW, at] = low
        hor[4 * RW : 6 * RW, at] = high

    for copy in halo:
        copy.wait_recv()
    down = jnp.dot(
        vertical, near[...].reshape(40, 1024), precision=lax.Precision.HIGHEST, preferred_element_type=F32
    )
    y_hi, y_lo = split(down)
    y_all = jnp.concatenate([y_hi, y_lo, y_hi], axis=1)
    def wait_for(ref, sem):
        pltpu.make_async_copy(ref, ref, sem).wait()

    most = pl.ds(0, 63)
    wait_for(given.at[most], par_sem.at[1])
    for e in range(64):
        params[2 * e : 2 * e + 2, :] = given[e]
    every = params[...]
    def field(k):
        return every[:, k : k + 1]

    profile = lax.broadcasted_iota(jnp.int32, (128, NPROF), 1).astype(F32)
    chosen = jnp.concatenate([jnp.where(profile == field(13 + b), 1.0, 0.0) for b in range(B)], axis=0)
    taken = jnp.dot(chosen, jnp.concatenate(box, axis=0), precision=lax.Precision.HIGHEST, preferred_element_type=F32)
    start = jnp.broadcast_to((field(1) - float(HALF)).astype(jnp.int32), (128, 128))
    start = jnp.concatenate([start] * B, axis=0)
    turn = jnp.concatenate([start] * 3, axis=1)
    for step in (1, 2, 4, 8, 16, 32, 64):
        if step == 64:
            taken = jnp.concatenate([taken, jnp.zeros((B * 128, RW), F32)], axis=1)
        taken = jnp.where((turn[:, 0 : taken.shape[1]] & step) != 0, pltpu.roll(taken, step, 1), taken)
    block = start >> 7
    spread = []
    for j in range(8):
        value = jnp.zeros((B * 128, RW), F32)
        for d in range(min(j, 2) + 1):
            value = jnp.where(block == j - d, taken[:, d * RW : (d + 1) * RW], value)
        spread.append(value)
    g_hi, g_lo = split(jnp.concatenate(spread, axis=1))
    caught = lax.dot_general(
        jnp.concatenate([g_hi, g_hi, g_lo], axis=1),
        y_all,
        (((1,), (1,)), ((), ())),
        preferred_element_type=F32,
    )
    place = lax.broadcasted_iota(jnp.int32, (128, 128), 1)
    offset = (me * 8 + (place >> 4)).astype(F32) - field(0)
    place = (place & 15).astype(F32)
    upper = (offset >= 0.0) & (offset < 128.0)
    lower = (offset >= 128.0) & (offset < 256.0)
    sum_of = jnp.zeros((128, 128), F32)
    for b in range(B):
        part = jnp.where(upper, field(7 + b), 0.0) + jnp.where(lower, field(10 + b), 0.0)
        sum_of = sum_of + jnp.where(place == field(16 + b), part, 0.0) * caught[b * 128 : (b + 1) * 128]
    model_sum = jnp.sum(sum_of.T, axis=0, keepdims=True)
    lane = lax.broadcasted_iota(jnp.int32, (1, 128), 1)
    parts[me] = jnp.where(lane == 2 * me, science_sum, 0.0) - model_sum

    def send_parts(k, carry):
        pltpu.make_async_remote_copy(
            src_ref=parts.at[me],
            dst_ref=parts.at[me],
            send_sem=lev_sem.at[0],
            recv_sem=lev_sem.at[1],
            device_id={"epoch": (me + k) & 63},
            device_id_type=MESH,
        ).start()
        return carry

    lax.fori_loop(1, 64, send_parts, 0, unroll=7)
    lax.fori_loop(FIRST, 64, send_science, 0, unroll=7)

    high, low = split(pltpu.roll(down, HALF, 1))

    def stacked(value):
        def block(j):
            return value[:, (j % 8) * RW : (j % 8 + 1) * RW]

        return jnp.concatenate(
            [jnp.concatenate([block(j), block(j + 1)], axis=1) for j in range(8)], axis=0
        )

    high, low = stacked(high), stacked(low)
    left = jnp.concatenate([high, high, low], axis=1)

    def make_pairs(step):
        both = jnp.dot(left, hor[:, step * 256 : (step + 1) * 256], preferred_element_type=F32)
        for half in range(2):
            q = 2 * step + half
            at = slice(q * NPROF, (q + 1) * NPROF)
            for j in range(8):
                cols = slice(j * RW, (j + 1) * RW)
                for r in range(8):
                    top = j * 128 + r * NPROF
                    pairs[r, at, cols] = both[top : top + NPROF, half * RW : (half + 1) * RW]

    for step in range(EARLY):
        make_pairs(step)

    across = every.T

    def entry(k):
        return across[k : k + 1, :]

    wait_for(parts.at[most], lev_sem.at[1])
    total = jnp.sum(parts[...], axis=0)
    even = (lane & 1) == 0
    total = total + jnp.where(even, pltpu.roll(total, 127, 1), pltpu.roll(total, 1, 1))
    sums[me_t] = jnp.concatenate([total * entry(3), entry(3)], axis=0)
    sum_copies = [
        pltpu.make_async_remote_copy(
            src_ref=sums.at[me_t],
            dst_ref=sums.at[me_t],
            send_sem=sum_send.at[k - 1],
            recv_sem=sum_recv.at[k - 1],
            device_id={"tile": (me_t + k) & 3},
            device_id_type=MESH,
        )
        for k in (1, 2, 3)
    ]
    for copy in sum_copies:
        copy.start()

    first = every[:, 1:2]
    column = lax.broadcasted_iota(jnp.int32, (128, 1024), 1).astype(F32)
    cover = jnp.where((column >= first) & (column < first + float(RW)), 1.0, 0.0).astype(BF16)
    my_row = (me * 8 + lax.broadcasted_iota(jnp.int32, (8, 128), 0)).astype(F32)
    inside = my_row - entry(0)
    upper = jnp.where((inside >= 0.0) & (inside < 128.0), 1.0, 0.0)
    lower = jnp.where((inside >= 128.0) & (inside < 256.0), 1.0, 0.0)

    pair_id = lax.broadcasted_iota(jnp.int32, (PAIRS, 128), 0).astype(F32)
    weight = [jnp.zeros((PAIRS, 128), F32)] * 2
    for b in range(B):
        same = pair_id == entry(4 + b)
        weight = [weight[y] + jnp.where(same, entry(7 + 3 * y + b), 0.0) for y in range(2)]

    def weight_of(r):
        return weight[0] * upper[r : r + 1, :] + weight[1] * lower[r : r + 1, :]

    for step in range(EARLY, NPROF // 2):
        make_pairs(step)
    column = lax.broadcasted_iota(jnp.int32, (8, 1024), 1).astype(F32)
    rows = (me * 8 + lax.broadcasted_iota(jnp.int32, (8, 1024), 0)).astype(F32)

    def make_mask(e, carry):
        top = jnp.broadcast_to(given[e, 0:1, 0:1], (8, 1024))
        side = jnp.broadcast_to(given[e, 0:1, 1:2], (8, 1024))
        hit = (rows >= top) & (rows < top + 256.0) & (column >= side) & (column < side + 256.0)
        masks[e] = jnp.where(hit, 1.0, 0.0)
        return carry

    lax.fori_loop(0, 64, make_mask, 0, unroll=4)

    for r in range(8):
        coef = wide_dot(weight_of(r) * entry(2), cover)
        model[r : r + 1, :] = jnp.sum(pairs[r] * coef, axis=0, keepdims=True)
    count = wide_dot((upper + lower) * entry(2), cover)
    scale = 1.0 / jnp.maximum(count, 1.0)

    wait_for(recv.at[most], sci_sem.at[1])

    def add_block(e, acc):
        halves = [recv[e, :, 0:RW], recv[e, :, RW : 2 * RW]]
        return [acc[k] + halves[k % 2] * masks[e, :, k * RW : (k + 1) * RW] for k in range(8)]

    acc = lax.fori_loop(0, 64, add_block, [jnp.zeros((8, RW), F32)] * 8, unroll=8)

    for copy in sum_copies:
        copy.wait_recv()
    both = (sums[0] + sums[1]) + (sums[2] + sums[3])
    level = both[0:1, :] / jnp.maximum(both[1:2, :] * 65536.0, 1.0)
    taken = model[...] + wide_dot((upper + lower) * (entry(2) * level), cover)
    for k in range(8):
        at = slice(k * RW, (k + 1) * RW)
        out[0, :, at] = (acc[k] - taken[:, at]) * scale[:, at]

    for copy in halo:
        copy.wait_send()
    for copy in sum_copies:
        copy.wait_send()
    wait_for(given.at[most], par_sem.at[0])
    wait_for(recv.at[most], sci_sem.at[0])
    wait_for(parts.at[most], lev_sem.at[0])


def on_device(
    coadd_image, science, row_offset, col_offset, intersections, visit_weight, basis_index, weights, profiles
):
    any_space = pl.BlockSpec(memory_space=pl.ANY)
    dma = pltpu.SemaphoreType.DMA
    return pl.pallas_call(
        kernel,
        out_shape=jax.ShapeDtypeStruct((1, 8, 1024), F32),
        in_specs=[any_space] * 9,
        out_specs=pl.BlockSpec(memory_space=pltpu.VMEM),
        scratch_shapes=[
            pltpu.VMEM((5, 8, 1024), F32),
            pltpu.VMEM((256, 256), F32),
            pltpu.VMEM((NPROF, KW), F32),
            pltpu.VMEM((NPROF, 2 * RW), F32),
            pltpu.VMEM((6 * RW, NPROF * RW), BF16),
            pltpu.VMEM((8, PAIRS, 1024), F32),
            pltpu.VMEM((32, 8, 256), F32),
            pltpu.VMEM((64, 8, 256), F32),
            pltpu.VMEM((64, 2, 128), F32),
            pltpu.VMEM((128, 128), F32),
            pltpu.VMEM((64, 8, 1024), F32),
            pltpu.VMEM((8, 1024), F32),
            pltpu.VMEM((64, 1, 128), F32),
            pltpu.VMEM((4, 2, 128), F32),
            pltpu.SMEM((1, 1), jnp.int32),
            pltpu.SMEM((1, 1), jnp.int32),
            pltpu.SMEM((1, 1), jnp.int32),
            pltpu.SMEM((1, 1), F32),
            pltpu.SMEM((1, 1, 2, 2, B), jnp.int32),
            pltpu.SMEM((1, 1, 2, 2, B), F32),
            dma((9,)),
            dma((4,)),
            dma((4,)),
            dma((3,)),
            dma((3,)),
            dma((2,)),
            dma((2,)),
            dma((2,)),
        ],
        compiler_params=pltpu.CompilerParams(
            collective_id=0, has_side_effects=True, vmem_limit_bytes=60 * 1024 * 1024
        ),
        name="difference",
    )(
        coadd_image, science, row_offset, col_offset, intersections, visit_weight,
        jnp.swapaxes(basis_index, 3, 4), weights, profiles,
    )


def solution(mesh):
    return jax.shard_map(
        on_device,
        mesh=mesh,
        in_specs=(
            P("tile", "epoch", None),
            P("tile", "epoch", None, None),
            P("tile", "epoch"),
            P("tile", "epoch"),
            P("tile", "epoch"),
            P("tile", "epoch"),
            P("tile", "epoch", None, None, None),
            P("tile", "epoch", None, None, None),
            P(),
        ),
        out_specs=P("tile", "epoch", None),
        check_vma=False,
    )
```

```python
import jax
import jax.numpy as jnp
from jax import lax
from jax.experimental import pallas as pl
from jax.experimental.pallas import tpu as pltpu
from jax.sharding import PartitionSpec as P

KW = 31
HALF = 15
RW = 128
B = 3
NPROF = 16
PAIRS = NPROF * NPROF
FIRST = 29
EARLY = 4
F32 = jnp.float32
BF16 = jnp.bfloat16
MESH = pl.DeviceIdType.MESH


def split(value):
    high = value.astype(BF16)
    return high, (value - high.astype(F32)).astype(BF16)


def roll_by(value, amount, axis):
    chosen = jnp.broadcast_to(amount, value.shape)
    step = 1
    while step < value.shape[axis]:
        value = jnp.where((chosen & step) != 0, pltpu.roll(value, step, axis), value)
        step *= 2
    return value


def wide_dot(a, b):
    high, low = split(a)
    return jnp.dot(
        jnp.concatenate([high, low], axis=1), jnp.concatenate([b, b], axis=0), preferred_element_type=F32
    )


def kernel(
    coadd, science, row_offset, col_offset, intersections, visit_weight, basis_index, weights, profiles,
    out,
    near, sci, prof, table, hor, pairs, slots, recv, given, params, masks, model,
    parts, sums,
    row_s, col_s, int_s, vis_s, bas_s, wei_s,
    local_sem, halo_send, halo_recv, sum_send, sum_recv, par_sem, sci_sem, lev_sem,
):
    me_t = lax.axis_index("tile")
    me = lax.axis_index("epoch")

    arrays = (
        (row_offset, row_s), (col_offset, col_s), (intersections, int_s), (visit_weight, vis_s),
        (basis_index, bas_s), (weights, wei_s), (profiles, prof),
    )
    small = [pltpu.make_async_copy(src, dst, local_sem.at[2 + i]) for i, (src, dst) in enumerate(arrays)]
    for copy in small:
        copy.start()
    sci_copy = pltpu.make_async_copy(science.at[0, 0], sci, local_sem.at[1])
    sci_copy.start()
    own_copy = pltpu.make_async_copy(coadd.at[0], near.at[2], local_sem.at[0])
    own_copy.start()

    barrier = pltpu.get_barrier_semaphore()

    def greet(k, carry):
        pl.semaphore_signal(barrier, inc=1, device_id={"epoch": (me + k) & 63}, device_id_type=MESH)
        return carry

    lax.fori_loop(1, 64, greet, 0, unroll=7)
    for k in (1, 2, 3):
        pl.semaphore_signal(barrier, inc=1, device_id={"tile": (me_t + k) & 3}, device_id_type=MESH)

    for copy in small:
        copy.wait()
    oy = row_s[0, 0]
    ox = col_s[0, 0]
    flag = int_s[0, 0].astype(F32)
    gain = flag * vis_s[0, 0]

    lane = lax.broadcasted_iota(jnp.int32, (2, 128), 1)
    region = lax.broadcasted_iota(jnp.int32, (2, 128), 0)

    def by_region(left, right):
        return jnp.where(region == 0, left, right)

    entries = [oy.astype(F32), by_region(ox.astype(F32), ox.astype(F32) + float(RW)), gain, flag]
    for b in range(B):
        pair = [(bas_s[0, 0, s, 0, b] * NPROF + bas_s[0, 0, s, 1, b]).astype(F32) for s in range(2)]
        entries.append(by_region(*pair))
    for y in range(2):
        for b in range(B):
            entries.append(by_region(wei_s[0, 0, y, 0, b], wei_s[0, 0, y, 1, b]))
    for pick in range(2):
        for b in range(B):
            entries.append(by_region(*[bas_s[0, 0, s, pick, b].astype(F32) for s in range(2)]))
    row = jnp.zeros((2, 128), F32)
    for k, entry in enumerate(entries):
        row = jnp.where(lane == k, entry, row)
    given[me] = row

    own_copy.wait()
    pl.semaphore_wait(barrier, 66)

    def send_params(k, carry):
        pltpu.make_async_remote_copy(
            src_ref=given.at[me],
            dst_ref=given.at[me],
            send_sem=par_sem.at[0],
            recv_sem=par_sem.at[1],
            device_id={"epoch": (me + k) & 63},
            device_id_type=MESH,
        ).start()
        return carry

    def send_science(k, carry):
        target = (me + 37 * k) & 63
        pltpu.make_async_remote_copy(
            src_ref=slots.at[(target & 31)],
            dst_ref=recv.at[me],
            send_sem=sci_sem.at[0],
            recv_sem=sci_sem.at[1],
            device_id={"epoch": target},
            device_id_type=MESH,
        ).start()
        return carry

    halo = [
        pltpu.make_async_remote_copy(
            src_ref=near.at[2],
            dst_ref=near.at[2 - d],
            send_sem=halo_send.at[i],
            recv_sem=halo_recv.at[i],
            device_id={"epoch": (me + d) & 63},
            device_id_type=MESH,
        )
        for i, d in enumerate((1, -1, 2, -2))
    ]
    for copy in halo:
        copy.start()
    lax.fori_loop(1, 64, send_params, 0, unroll=7)

    sci_copy.wait()
    image = sci[...]
    science_sum = jnp.sum(image)
    slots[...] = (roll_by(roll_by(image, ox & 255, 1), oy & 255, 0) * gain).reshape(32, 8, 256)
    lax.fori_loop(1, FIRST, send_science, 0, unroll=7)
    recv[me] = slots[(me & 31)]

    table[...] = jnp.zeros_like(table)
    table[:, 0:KW] = prof[...]
    wide = table[:, 0:128]
    vertical = jnp.concatenate([pltpu.roll(wide, r + 1, 1) for r in range(8)], axis=0)[:, 0:40]
    box = []
    for q in range(NPROF):
        band = pltpu.roll(
            jnp.broadcast_to(table[q : q + 1, :], (RW, 2 * RW)), 0, 1, stride=1, stride_axis=0
        )
        box.append(jnp.sum(band, axis=0, keepdims=True))
        high, low = split(band.T)
        at = slice(q * RW, (q + 1) * RW)
        hor[0 : 2 * RW, at] = high
        hor[2 * RW : 4 * RW, at] = low
        hor[4 * RW : 6 * RW, at] = high

    for copy in halo:
        copy.wait_recv()
    down = jnp.dot(
        vertical, near[...].reshape(40, 1024), precision=lax.Precision.HIGHEST, preferred_element_type=F32
    )
    y_hi, y_lo = split(down)
    y_all = jnp.concatenate([y_hi, y_lo, y_hi], axis=1)
    def wait_for(ref, sem):
        pltpu.make_async_copy(ref, ref, sem).wait()

    most = pl.ds(0, 63)
    wait_for(given.at[most], par_sem.at[1])
    for e in range(64):
        params[2 * e : 2 * e + 2, :] = given[e]
    every = params[...]
    def field(k):
        return every[:, k : k + 1]

    profile = lax.broadcasted_iota(jnp.int32, (128, NPROF), 1).astype(F32)
    chosen = jnp.concatenate([jnp.where(profile == field(13 + b), 1.0, 0.0) for b in range(B)], axis=0)
    taken = jnp.dot(chosen, jnp.concatenate(box, axis=0), precision=lax.Precision.HIGHEST, preferred_element_type=F32)
    start = jnp.broadcast_to((field(1) - float(HALF)).astype(jnp.int32), (128, 128))
    start = jnp.concatenate([start] * B, axis=0)
    turn = jnp.concatenate([start] * 3, axis=1)
    for step in (1, 2, 4, 8, 16, 32, 64):
        if step == 64:
            taken = jnp.concatenate([taken, jnp.zeros((B * 128, RW), F32)], axis=1)
        taken = jnp.where((turn[:, 0 : taken.shape[1]] & step) != 0, pltpu.roll(taken, step, 1), taken)
    block = start >> 7
    spread = []
    for j in range(8):
        value = jnp.zeros((B * 128, RW), F32)
        for d in range(min(j, 2) + 1):
            value = jnp.where(block == j - d, taken[:, d * RW : (d + 1) * RW], value)
        spread.append(value)
    g_hi, g_lo = split(jnp.concatenate(spread, axis=1))
    caught = lax.dot_general(
        jnp.concatenate([g_hi, g_hi, g_lo], axis=1),
        y_all,
        (((1,), (1,)), ((), ())),
        preferred_element_type=F32,
    )
    place = lax.broadcasted_iota(jnp.int32, (128, 128), 1)
    offset = (me * 8 + (place >> 4)).astype(F32) - field(0)
    place = (place & 15).astype(F32)
    upper = (offset >= 0.0) & (offset < 128.0)
    lower = (offset >= 128.0) & (offset < 256.0)
    sum_of = jnp.zeros((128, 128), F32)
    for b in range(B):
        part = jnp.where(upper, field(7 + b), 0.0) + jnp.where(lower, field(10 + b), 0.0)
        sum_of = sum_of + jnp.where(place == field(16 + b), part, 0.0) * caught[b * 128 : (b + 1) * 128]
    model_sum = jnp.sum(sum_of.T, axis=0, keepdims=True)
    lane = lax.broadcasted_iota(jnp.int32, (1, 128), 1)
    parts[me] = jnp.where(lane == 2 * me, science_sum, 0.0) - model_sum

    def send_parts(k, carry):
        pltpu.make_async_remote_copy(
            src_ref=parts.at[me],
            dst_ref=parts.at[me],
            send_sem=lev_sem.at[0],
            recv_sem=lev_sem.at[1],
            device_id={"epoch": (me + k) & 63},
            device_id_type=MESH,
        ).start()
        return carry

    lax.fori_loop(1, 64, send_parts, 0, unroll=7)
    lax.fori_loop(FIRST, 64, send_science, 0, unroll=7)

    high, low = split(pltpu.roll(down, HALF, 1))

    def stacked(value):
        def block(j):
            return value[:, (j % 8) * RW : (j % 8 + 1) * RW]

        return jnp.concatenate(
            [jnp.concatenate([block(j), block(j + 1)], axis=1) for j in range(8)], axis=0
        )

    high, low = stacked(high), stacked(low)
    left = jnp.concatenate([high, high, low], axis=1)

    def make_pairs(step):
        both = jnp.dot(left, hor[:, step * 256 : (step + 1) * 256], preferred_element_type=F32)
        for half in range(2):
            q = 2 * step + half
            at = slice(q * NPROF, (q + 1) * NPROF)
            for j in range(8):
                cols = slice(j * RW, (j + 1) * RW)
                for r in range(8):
                    top = j * 128 + r * NPROF
                    pairs[r, at, cols] = both[top : top + NPROF, half * RW : (half + 1) * RW]

    for step in range(EARLY):
        make_pairs(step)

    across = every.T

    def entry(k):
        return across[k : k + 1, :]

    wait_for(parts.at[most], lev_sem.at[1])
    total = jnp.sum(parts[...], axis=0)
    even = (lane & 1) == 0
    total = total + jnp.where(even, pltpu.roll(total, 127, 1), pltpu.roll(total, 1, 1))
    sums[me_t] = jnp.concatenate([total * entry(3), entry(3)], axis=0)
    sum_copies = [
        pltpu.make_async_remote_copy(
            src_ref=sums.at[me_t],
            dst_ref=sums.at[me_t],
            send_sem=sum_send.at[k - 1],
            recv_sem=sum_recv.at[k - 1],
            device_id={"tile": (me_t + k) & 3},
            device_id_type=MESH,
        )
        for k in (1, 2, 3)
    ]
    for copy in sum_copies:
        copy.start()

    first = every[:, 1:2]
    column = lax.broadcasted_iota(jnp.int32, (128, 1024), 1).astype(F32)
    cover = jnp.where((column >= first) & (column < first + float(RW)), 1.0, 0.0).astype(BF16)
    my_row = (me * 8 + lax.broadcasted_iota(jnp.int32, (8, 128), 0)).astype(F32)
    inside = my_row - entry(0)
    upper = jnp.where((inside >= 0.0) & (inside < 128.0), 1.0, 0.0)
    lower = jnp.where((inside >= 128.0) & (inside < 256.0), 1.0, 0.0)

    pair_id = lax.broadcasted_iota(jnp.int32, (PAIRS, 128), 0).astype(F32)
    weight = [jnp.zeros((PAIRS, 128), F32)] * 2
    for b in range(B):
        same = pair_id == entry(4 + b)
        weight = [weight[y] + jnp.where(same, entry(7 + 3 * y + b), 0.0) for y in range(2)]

    def weight_of(r):
        return weight[0] * upper[r : r + 1, :] + weight[1] * lower[r : r + 1, :]

    for step in range(EARLY, NPROF // 2):
        make_pairs(step)
    column = lax.broadcasted_iota(jnp.int32, (8, 1024), 1).astype(F32)
    rows = (me * 8 + lax.broadcasted_iota(jnp.int32, (8, 1024), 0)).astype(F32)

    def make_mask(e, carry):
        top = jnp.broadcast_to(given[e, 0:1, 0:1], (8, 1024))
        side = jnp.broadcast_to(given[e, 0:1, 1:2], (8, 1024))
        hit = (rows >= top) & (rows < top + 256.0) & (column >= side) & (column < side + 256.0)
        masks[e] = jnp.where(hit, 1.0, 0.0)
        return carry

    lax.fori_loop(0, 64, make_mask, 0, unroll=4)

    for r in range(8):
        coef = wide_dot(weight_of(r) * entry(2), cover)
        model[r : r + 1, :] = jnp.sum(pairs[r] * coef, axis=0, keepdims=True)
    count = wide_dot((upper + lower) * entry(2), cover)
    scale = 1.0 / jnp.maximum(count, 1.0)

    wait_for(recv.at[most], sci_sem.at[1])

    def add_block(e, acc):
        halves = [recv[e, :, 0:RW], recv[e, :, RW : 2 * RW]]
        return [acc[k] + halves[k % 2] * masks[e, :, k * RW : (k + 1) * RW] for k in range(8)]

    acc = lax.fori_loop(0, 64, add_block, [jnp.zeros((8, RW), F32)] * 8, unroll=8)

    for copy in sum_copies:
        copy.wait_recv()
    both = (sums[0] + sums[1]) + (sums[2] + sums[3])
    level = both[0:1, :] / jnp.maximum(both[1:2, :] * 65536.0, 1.0)
    taken = model[...] + wide_dot((upper + lower) * (entry(2) * level), cover)
    for k in range(8):
        at = slice(k * RW, (k + 1) * RW)
        out[0, :, at] = (acc[k] - taken[:, at]) * scale[:, at]

    for copy in halo:
        copy.wait_send()
    for copy in sum_copies:
        copy.wait_send()
    wait_for(given.at[most], par_sem.at[0])
    wait_for(recv.at[most], sci_sem.at[0])
    wait_for(parts.at[most], lev_sem.at[0])


def on_device(
    coadd_image, science, row_offset, col_offset, intersections, visit_weight, basis_index, weights, profiles
):
    any_space = pl.BlockSpec(memory_space=pl.ANY)
    dma = pltpu.SemaphoreType.DMA
    return pl.pallas_call(
        kernel,
        out_shape=jax.ShapeDtypeStruct((1, 8, 1024), F32),
        in_specs=[any_space] * 9,
        out_specs=pl.BlockSpec(memory_space=pltpu.VMEM),
        scratch_shapes=[
            pltpu.VMEM((5, 8, 1024), F32),
            pltpu.VMEM((256, 256), F32),
            pltpu.VMEM((NPROF, KW), F32),
            pltpu.VMEM((NPROF, 2 * RW), F32),
            pltpu.VMEM((6 * RW, NPROF * RW), BF16),
            pltpu.VMEM((8, PAIRS, 1024), F32),
            pltpu.VMEM((32, 8, 256), F32),
            pltpu.VMEM((64, 8, 256), F32),
            pltpu.VMEM((64, 2, 128), F32),
            pltpu.VMEM((128, 128), F32),
            pltpu.VMEM((64, 8, 1024), F32),
            pltpu.VMEM((8, 1024), F32),
            pltpu.VMEM((64, 1, 128), F32),
            pltpu.VMEM((4, 2, 128), F32),
            pltpu.SMEM((1, 1), jnp.int32),
            pltpu.SMEM((1, 1), jnp.int32),
            pltpu.SMEM((1, 1), jnp.int32),
            pltpu.SMEM((1, 1), F32),
            pltpu.SMEM((1, 1, 2, 2, B), jnp.int32),
            pltpu.SMEM((1, 1, 2, 2, B), F32),
            dma((9,)),
            dma((4,)),
            dma((4,)),
            dma((3,)),
            dma((3,)),
            dma((2,)),
            dma((2,)),
            dma((2,)),
        ],
        compiler_params=pltpu.CompilerParams(
            collective_id=0, has_side_effects=True, vmem_limit_bytes=60 * 1024 * 1024
        ),
        name="difference",
    )(
        coadd_image, science, row_offset, col_offset, intersections, visit_weight,
        jnp.swapaxes(basis_index, 3, 4), weights, profiles,
    )


def solution(mesh):
    return jax.shard_map(
        on_device,
        mesh=mesh,
        in_specs=(
            P("tile", "epoch", None),
            P("tile", "epoch", None, None),
            P("tile", "epoch"),
            P("tile", "epoch"),
            P("tile", "epoch"),
            P("tile", "epoch"),
            P("tile", "epoch", None, None, None),
            P("tile", "epoch", None, None, None),
            P(),
        ),
        out_specs=P("tile", "epoch", None),
        check_vma=False,
    )
```
